512 devices in a mesh: col: 16 (over x_hi, y, core), fac: 32 (over x_lo, z).
Axes of the slice: x: 4 (x_hi: 2, x_lo: 2; x = x_hi * 2 + x_lo), y: 4, z: 16, core: 2. Of those that a mesh axis runs over, the one named last changes fastest.
Arguments:
- facets: bfloat16 [2, 4096, 4096], P(None, 'col', 'fac'), may hold values from -6 to 6
- row_taper: float32 [4096], P('col'), may hold values from 0.5 to 1.5
- column_taper: float32 [4096], replicated, may hold values from 0.5 to 1.5
- column_place: int32 [1], replicated, may hold values from 0 to 511
- row_offset: int32 [16], replicated, may hold values from 0 to 4095
- column_offset: int32 [32], replicated, may hold values from 0 to 4095
- slot_subgrid: int32 [16, 32], replicated, may hold values from 0 to 31, each once within a row
Outputs:
- subgrids: float32 [16, 32, 2, 512, 128], P('col', 'fac')
The draws below stay inside these ranges and needn't reach their ends.
All inputs are finite; a program needn't handle non-finite values.
Results may differ from the reference program's by a relative error of at most 0.0052.
Values may be sent and summed in bfloat16 or wider, within the bound.
No kernel may reach another device: no remote copies, remote signals or barrier semaphores. Data moves between devices by JAX's collectives and lax.ppermute only.
A program may use at most 64 MiB of HBM per device.

```python
import math
import jax
import jax.numpy as jnp
from jax import lax

FACET = 4096
STRIP = 128
SUBGRID = 512
FACET_COLS = 1
IMG_COLS = 4096
N_COL = 16
N_FAC = 32


def touch_ends(drawn, key, low, high):
    longest = drawn.shape.index(max(drawn.shape))
    spots = []
    for shift in (0, 1):
        where = [jax.random.randint(jax.random.fold_in(key, axis), (), 0, length) for axis, length in enumerate(drawn.shape)]
        where[longest] = (where[longest] + shift) % drawn.shape[longest]
        spots.append(tuple(where))
    return drawn.at[spots[0]].set(low).at[spots[1]].set(high)


def level_of(own_key, dims, cuts, least, high):
    factor_of, own = 1.0, jax.random.fold_in(own_key, 6)
    for position, blocks in cuts:
        heights = jnp.exp(jax.random.uniform(jax.random.fold_in(own, position), (blocks,), jnp.float32, least / len(cuts), high / len(cuts)))
        factor_of = factor_of * jnp.repeat(heights, dims[position] // blocks).reshape([-1 if axis == position else 1 for axis in range(len(dims))])
    return factor_of


def centred(key, extent, scale, bound, split=(), held_as=jnp.bfloat16):
    gain = level_of(key, extent, split, -0.22, 0.18) if split else 1.0
    result = jax.random.normal(key, extent, jnp.float32) * scale * gain
    return jnp.minimum(jnp.maximum(result, -bound), bound).astype(held_as)


def setup_inputs(seed: int = 0) -> dict:
    keys = jax.random.split(jax.random.key(seed), 8)
    facets = centred(keys[0], (2, FACET, IMG_COLS), 1.0, 6.0, ((1, 16), (2, 32)))
    row_taper = jnp.clip(0.5 + 1.0 * jax.random.uniform(keys[1], (FACET,), jnp.float32) ** level_of(keys[1], (FACET,), ((0, 16),), -0.2, 0.2), 0.5, 1.5)
    column_taper = jnp.clip(jax.random.uniform(keys[2], (FACET,), jnp.float32, 0.5, 1.5), 0.5, 1.5)
    column_place = jax.random.randint(keys[3], (FACET_COLS,), 0, SUBGRID).astype(jnp.int32)
    row_offset = touch_ends(jax.random.randint(keys[4], (N_COL,), 0, FACET), jax.random.fold_in(keys[4], 1), 0, FACET - 1).astype(jnp.int32)
    column_offset = touch_ends(jax.random.randint(keys[5], (N_FAC,), 0, FACET), jax.random.fold_in(keys[5], 1), 0, FACET - 1).astype(jnp.int32)
    slot_subgrid = jax.vmap(lambda own: jax.random.permutation(own, N_FAC))(jax.random.split(keys[6], N_COL)).reshape((N_COL, N_FAC)).astype(jnp.int32)
    return {"facets": facets, "row_taper": row_taper, "column_taper": column_taper, "column_place": column_place, "row_offset": row_offset, "column_offset": column_offset, "slot_subgrid": slot_subgrid}


def phase_table(starts, positions):
    offsets = jnp.arange(STRIP, dtype=jnp.int32)
    frequency = (starts[:, None] + offsets[None, :]) % FACET
    phases = frequency[:, :, None] * positions[None, None, :] % FACET
    angles = phases.astype(jnp.float32) * (2.0 * math.pi / FACET)
    norm_scale = 1.0 / math.sqrt(FACET)
    return jnp.stack([jnp.cos(angles) * norm_scale, -jnp.sin(angles) * norm_scale]).astype(jnp.bfloat16)

def complex_rows(table_rows, real_part, imag_part):
    row_total = table_rows.shape[1]
    stacked = table_rows.reshape(2 * row_total, table_rows.shape[2])
    first_product = jnp.dot(stacked, real_part, preferred_element_type=jnp.float32)
    second = jnp.dot(stacked, imag_part, preferred_element_type=jnp.float32)
    return (first_product[:row_total] - second[row_total:], second[:row_total] + first_product[row_total:])

def complex_cols(table_rows, real_part, imag_part):
    row_total = table_rows.shape[1]
    stacked = table_rows.reshape(2 * row_total, table_rows.shape[2])
    contract_dims = (((1,), (1,)), ((), ()))
    first_product = lax.dot_general(stacked, real_part, contract_dims, preferred_element_type=jnp.float32)
    second = lax.dot_general(stacked, imag_part, contract_dims, preferred_element_type=jnp.float32)
    return (first_product[:row_total] - second[row_total:], second[:row_total] + first_product[row_total:])

def reference(facets, row_taper, column_taper, column_place, row_offset, column_offset, slot_subgrid):
    column_gain = jnp.tile(column_taper, FACET_COLS)
    prepared = (facets.astype(jnp.float32) * row_taper[None, :, None] * column_gain[None, None, :]).astype(jnp.bfloat16)
    positions = jnp.arange(FACET, dtype=jnp.int32)
    offsets = jnp.arange(STRIP, dtype=jnp.int32)
    column_targets = (column_place[:, None] + offsets[None, :]) % SUBGRID

    def one_group(column_group):
        encode = phase_table(row_offset[column_group][None], positions)[:, 0]
        real_out, imag_out = complex_rows(encode, prepared[0], prepared[1])
        strip = lax.optimization_barrier(jnp.stack([real_out, imag_out]).astype(jnp.bfloat16))
        starts = column_offset[slot_subgrid[column_group]]
        decode = phase_table(starts, positions).reshape(2, N_FAC * STRIP, FACET)

        def add_facet(summed, facet_col):
            part_real = lax.dynamic_slice_in_dim(strip[0], facet_col * FACET, FACET, 1)
            part_imag = lax.dynamic_slice_in_dim(strip[1], facet_col * FACET, FACET, 1)
            real_part, imag_part = complex_cols(decode, part_real, part_imag)
            contribution = jnp.stack([real_part.reshape(N_FAC, STRIP, STRIP), imag_part.reshape(N_FAC, STRIP, STRIP)], axis=1)
            summed = summed.at[:, :, column_targets[facet_col], :].add(contribution)
            return (summed, None)
        summed, unused = lax.scan(add_facet, jnp.zeros((N_FAC, 2, SUBGRID, STRIP), jnp.float32), jnp.arange(FACET_COLS, dtype=jnp.int32))
        return summed
    return lax.map(one_group, jnp.arange(N_COL, dtype=jnp.int32))
```

```python
import math

import jax
import jax.numpy as jnp
import numpy as np
from jax import lax
from jax.experimental import pallas as pl
from jax.experimental.pallas import tpu as pltpu
from jax.sharding import Mesh, PartitionSpec as P

FACET = 4096
STRIP = 128
SUBGRID = 512
HALF = 256
SPLIT = ("xh", "y", "core", "xl", "zh", "zl")
SIZES = (2, 4, 2, 2, 4, 4)
COL = SPLIT[:3]
FAC = SPLIT[3:]
F32 = jnp.float32
BF16 = jnp.bfloat16
VMEM = pl.BlockSpec(memory_space=pltpu.VMEM)
SMEM = pl.BlockSpec(memory_space=pltpu.SMEM)
NT = (((1,), (1,)), ((), ()))


def base_table():
    k = np.arange(STRIP)[:, None]
    j = np.arange(HALF)[None, :]
    angle = (k * j % FACET) * (2.0 * math.pi / FACET)
    scale = 1.0 / math.sqrt(FACET)
    return np.stack([np.cos(angle) * scale, -np.sin(angle) * scale]).astype(np.float32)


def unit(phase):
    angle = phase.astype(F32) * (2.0 * math.pi / FACET)
    return jnp.cos(angle), -jnp.sin(angle)


def turned(base_ref, turned_ref, block):
    k = lax.broadcasted_iota(jnp.int32, (16, HALF), 0)
    real, imag = unit((k * block & 15) * HALF)
    for row in range(0, STRIP, 16):
        rows = pl.ds(row, 16)
        base_real, base_imag = base_ref[0, rows, :], base_ref[1, rows, :]
        turned_ref[0, rows, :] = base_real * real - base_imag * imag
        turned_ref[1, rows, :] = base_real * imag + base_imag * real


def fill_tables(starts, blocks, base_ref, out_ref, turned_ref):
    count = len(starts)
    padded = 8
    row = lax.broadcasted_iota(jnp.int32, (padded, HALF), 0)
    lane = lax.broadcasted_iota(jnp.int32, (padded, HALF), 1)
    first = jnp.zeros((padded, HALF), jnp.int32)
    for n, start in enumerate(starts):
        first = jnp.where(row == n, start, first)
    for c, block in enumerate(blocks):
        turned(base_ref, turned_ref, block)
        real, imag = unit(first * (block * HALF + lane) & (FACET - 1))
        for k in range(0, STRIP, 16):
            rows = pl.ds(k, 16)
            base_real, base_imag = turned_ref[0, rows, :], turned_ref[1, rows, :]
            for n in range(count):
                own_real, own_imag = real[n : n + 1], imag[n : n + 1]
                out_ref[n, rows, HALF * c : HALF * (c + 1)] = (
                    own_real * base_real - own_imag * base_imag
                ).astype(BF16)
                out_ref[n, pl.ds(STRIP + k, 16), HALF * c : HALF * (c + 1)] = (
                    own_real * base_imag + own_imag * base_real
                ).astype(BF16)


def prepare_kernel(facets_ref, row_ref, column_ref, out_ref):
    fac = (lax.axis_index("xl") * 4 + lax.axis_index("zh")) * 4 + lax.axis_index("zl")
    column = column_ref[pl.ds(fac, 1), :]
    for part in range(2):
        scaled = facets_ref[part].astype(F32) * column
        out_ref[STRIP * part : STRIP * (part + 1), :] = (scaled.T * row_ref[...]).astype(BF16)


def encode_kernel(row_offset_ref, base_ref, out_ref, turned_ref):
    core = lax.axis_index("core")
    pair = lax.axis_index("xh") * 4 + lax.axis_index("y")
    starts = [row_offset_ref[2 * n + core] for n in range(8)]
    fill_tables(starts, [2 * pair + core, 2 * pair + 1 - core], base_ref, out_ref, turned_ref)


def decode_kernel(slot_ref, offset_ref, base_ref, out_ref, turned_ref):
    column = (lax.axis_index("xh") * 4 + lax.axis_index("y")) * 2 + lax.axis_index("core")
    zh = lax.axis_index("zh")
    slot = lax.axis_index("xl") * 16 + lax.axis_index("zl")
    starts = [offset_ref[slot_ref[column, slot + 4 * n]] for n in range(4)]
    blocks = [2 * zh, 2 * zh + 1, 2 * zh + 8, 2 * zh + 9]
    fill_tables(starts, blocks, base_ref, out_ref, turned_ref)


def strip_kernel(own_ref, other_ref, table_ref, out_ref):
    for n in range(8):
        product = lax.dot_general(
            own_ref[...], table_ref[n, :, :HALF], NT, preferred_element_type=F32
        ) + lax.dot_general(
            other_ref[...], table_ref[n, :, HALF:], NT, preferred_element_type=F32
        )
        out_ref[n, :, :STRIP] = (product[:STRIP, :STRIP] - product[STRIP:, STRIP:]).astype(BF16)
        out_ref[n, :, STRIP:] = (product[:STRIP, STRIP:] + product[STRIP:, :STRIP]).astype(BF16)


def sum_kernel(parts_ref, out_ref):
    total = parts_ref[0].astype(F32)
    for n in range(1, 8):
        total += parts_ref[n].astype(F32)
    total = total.astype(BF16)
    for n in range(8):
        out_ref[n] = total


def subgrid_kernel(strip_ref, table_ref, out_ref):
    strip = strip_ref[...].reshape(8 * STRIP, 2 * STRIP)
    for n in range(4):
        product = jnp.dot(table_ref[n], strip, preferred_element_type=F32)
        out_ref[n, :STRIP] = (product[:STRIP, :STRIP] - product[STRIP:, STRIP:]).astype(BF16)
        out_ref[n, STRIP:] = (product[:STRIP, STRIP:] + product[STRIP:, :STRIP]).astype(BF16)


def place_kernel(place_ref, parts_ref, out_ref, scratch_ref):
    place = place_ref[0] & (SUBGRID - 1)
    scratch_ref[...] = jnp.zeros_like(scratch_ref)
    for part in range(2):
        rows = slice(STRIP * part, STRIP * (part + 1))
        total = parts_ref[0, rows, :].astype(F32)
        for n in range(1, 4):
            total += parts_ref[n, rows, :].astype(F32)
        scratch_ref[part, pl.ds(place, STRIP), :] = total
    out_ref[:, STRIP:, :] = scratch_ref[:, STRIP:SUBGRID, :]
    out_ref[:, :STRIP, :] = scratch_ref[:, :STRIP, :] + scratch_ref[:, SUBGRID:, :]


def call(kernel, specs, shape, dtype, scratch=(), flops=0, moved=1 << 20):
    return pl.pallas_call(
        kernel,
        out_shape=jax.ShapeDtypeStruct(shape, dtype),
        in_specs=specs,
        out_specs=VMEM,
        scratch_shapes=list(scratch),
        compiler_params=pltpu.CompilerParams(vmem_limit_bytes=24 * 1024 * 1024),
        cost_estimate=pl.CostEstimate(flops=flops, bytes_accessed=moved, transcendentals=0),
    )


def on_device(
    facets, row_taper, column_taper, column_place, row_offset, column_offset, slot_subgrid
):
    base = jnp.asarray(base_table())
    turned_scratch = pltpu.VMEM((2, STRIP, HALF), F32)
    own = call(prepare_kernel, [VMEM] * 3, (2 * STRIP, HALF), BF16)(
        facets, row_taper.reshape(1, HALF), column_taper.reshape(32, STRIP)
    )
    other = lax.ppermute(own, "core", [(0, 1), (1, 0)])
    encode = call(
        encode_kernel, [SMEM, VMEM], (8, 2 * STRIP, 2 * HALF), BF16, [turned_scratch], moved=3 << 20
    )(row_offset, base)
    decode = call(
        decode_kernel, [SMEM, SMEM, VMEM], (4, 2 * STRIP, 4 * HALF), BF16, [turned_scratch], moved=3 << 20
    )(slot_subgrid, column_offset, base)
    shares = call(strip_kernel, [VMEM] * 3, (8, STRIP, 2 * STRIP), BF16, flops=1 << 29)(
        own, other, encode
    )
    shares = lax.all_to_all(shares, ("xh", "y"), 0, 0)
    strip = call(sum_kernel, [VMEM], (8, STRIP, 2 * STRIP), BF16)(shares)
    strips = lax.all_to_all(strip, ("xl", "zl"), 0, 0)
    partial = call(subgrid_kernel, [VMEM] * 2, (4, 2 * STRIP, STRIP), BF16, flops=1 << 29)(
        strips, decode
    )
    received = lax.all_to_all(partial, "zh", 0, 0)
    subgrid = call(
        place_kernel,
        [SMEM, VMEM],
        (2, SUBGRID, STRIP),
        F32,
        [pltpu.VMEM((2, SUBGRID + STRIP, STRIP), F32)],
    )(column_place, received)
    return subgrid.reshape(1, 1, 2, SUBGRID, STRIP)


def solution(mesh):
    split = Mesh(mesh.devices.reshape(SIZES), SPLIT)
    in_specs = (P(None, COL, FAC), P(COL), P(), P(), P(), P(), P())
    return jax.shard_map(
        on_device,
        mesh=split,
        in_specs=in_specs,
        out_specs=P(COL, FAC, None, None, None),
        check_vma=False,
    )
```

```python
import functools
import math

import jax
import jax.numpy as jnp
import numpy as np
from jax import lax
from jax.experimental import pallas as pl
from jax.experimental.pallas import tpu as pltpu
from jax.sharding import Mesh, PartitionSpec as P

FACET = 4096
STRIP = 128
SUBGRID = 512
HALF = 256
SPLIT = ("xh", "y", "core", "xl", "zh", "zl")
SIZES = (2, 4, 2, 2, 4, 4)
COL = SPLIT[:3]
FAC = SPLIT[3:]
F32 = jnp.float32
BF16 = jnp.bfloat16
VMEM = pl.BlockSpec(memory_space=pltpu.VMEM)
HBM = pl.BlockSpec(memory_space=pltpu.HBM)
SMEM = pl.BlockSpec(memory_space=pltpu.SMEM)
ENCODE = slice(2 * STRIP, 2 * STRIP + 8)
DECODE = slice(2 * STRIP + 8, 2 * STRIP + 16)
NT = (((1,), (1,)), ((), ()))


def base_table():
    k = np.arange(STRIP)[:, None]
    j = np.arange(HALF)[None, :]
    angle = (k * j % FACET) * (2.0 * math.pi / FACET)
    scale = 1.0 / math.sqrt(FACET)
    return np.stack([np.cos(angle) * scale, -np.sin(angle) * scale]).astype(np.float32)


def unit(phase):
    angle = phase.astype(F32) * (2.0 * math.pi / FACET)
    return jnp.cos(angle), -jnp.sin(angle)


def turned(pack_ref, turned_ref, block):
    k = lax.broadcasted_iota(jnp.int32, (16, HALF), 0)
    real, imag = unit((k * block & 15) * HALF)
    for row in range(0, STRIP, 16):
        rows = pl.ds(row, 16)
        base_real, base_imag = pack_ref[rows, :], pack_ref[pl.ds(STRIP + row, 16), :]
        turned_ref[0, rows, :] = base_real * real - base_imag * imag
        turned_ref[1, rows, :] = base_real * imag + base_imag * real


def spread(starts):
    row = lax.broadcasted_iota(jnp.int32, (8, HALF), 0)
    first = jnp.zeros((8, HALF), jnp.int32)
    for n, start in enumerate(starts):
        first = jnp.where(row == n, start, first)
    return first.astype(F32)


def fill_tables(pack_ref, firsts, count, blocks, out_ref, turned_ref):
    lane = lax.broadcasted_iota(jnp.int32, (8, HALF), 1)
    first = pack_ref[firsts].astype(jnp.int32)
    for c, block in enumerate(blocks):
        turned(pack_ref, turned_ref, block)
        real, imag = unit(first * (block * HALF + lane) & (FACET - 1))
        for k in range(0, STRIP, 16):
            rows = pl.ds(k, 16)
            base_real, base_imag = turned_ref[0, rows, :], turned_ref[1, rows, :]
            for n in range(count):
                own_real, own_imag = real[n : n + 1], imag[n : n + 1]
                out_ref[n, rows, HALF * c : HALF * (c + 1)] = (
                    own_real * base_real - own_imag * base_imag
                ).astype(BF16)
                out_ref[n, pl.ds(STRIP + k, 16), HALF * c : HALF * (c + 1)] = (
                    own_real * base_imag + own_imag * base_real
                ).astype(BF16)


def prepare_kernel(
    facets_hbm,
    row_hbm,
    column_hbm,
    row_offset_hbm,
    offset_hbm,
    slot_hbm,
    base_hbm,
    out_ref,
    pack_ref,
    facets_ref,
    row_ref,
    column_ref,
    row_offset_ref,
    offset_ref,
    slot_ref,
    sems,
):
    copies = [
        pltpu.make_async_copy(source, target, sems.at[n])
        for n, (source, target) in enumerate(
            [
                (facets_hbm, facets_ref),
                (row_hbm, row_ref),
                (column_hbm, column_ref),
                (row_offset_hbm, row_offset_ref),
                (offset_hbm, offset_ref),
                (slot_hbm, slot_ref),
                (base_hbm, pack_ref.at[pl.ds(0, 2 * STRIP)]),
            ]
        )
    ]
    for copy in copies:
        copy.start()
    core, xl, zh, zl = (lax.axis_index(name) for name in ("core", "xl", "zh", "zl"))
    pair = lax.axis_index("xh") * 4 + lax.axis_index("y")
    for copy in copies[3:6]:
        copy.wait()
    pack_ref[ENCODE] = spread([row_offset_ref[2 * n + core] for n in range(8)])
    pack_ref[DECODE] = spread(
        [
            offset_ref[slot_ref[2 * pair + core, 16 * xl + 4 * n + ((zl - zh + n) & 3)] & 31]
            for n in range(4)
        ]
    )
    for copy in copies[:3]:
        copy.wait()
    column = column_ref[pl.ds((xl * 4 + zh) * 4 + zl, 1), :]
    for part in range(2):
        scaled = facets_ref[part].astype(F32) * column
        out_ref[STRIP * part : STRIP * (part + 1), :] = (scaled.T * row_ref[...]).astype(BF16)
    copies[6].wait()


def encode_kernel(pack_ref, out_ref, turned_ref):
    core = lax.axis_index("core")
    pair = lax.axis_index("xh") * 4 + lax.axis_index("y")
    fill_tables(pack_ref, ENCODE, 8, [2 * pair + core, 2 * pair + 1 - core], out_ref, turned_ref)


def decode_kernel(xl, pack_ref, out_ref, turned_ref):
    block = 8 * xl + 2 * lax.axis_index("zh")
    fill_tables(pack_ref, DECODE, 4, [block, block + 1], out_ref, turned_ref)


def strip_kernel(own_ref, other_ref, table_ref, out_ref):
    for n in range(8):
        product = lax.dot_general(
            own_ref[...], table_ref[n, :, :HALF], NT, preferred_element_type=F32
        ) + lax.dot_general(
            other_ref[...], table_ref[n, :, HALF:], NT, preferred_element_type=F32
        )
        out_ref[n, :, :STRIP] = (product[:STRIP, :STRIP] - product[STRIP:, STRIP:]).astype(BF16)
        out_ref[n, :, STRIP:] = (product[:STRIP, STRIP:] + product[STRIP:, :STRIP]).astype(BF16)


def sum_kernel(parts_ref, out_ref):
    total = parts_ref[0].astype(F32)
    for n in range(1, 8):
        total += parts_ref[n].astype(F32)
    total = total.astype(BF16)
    for n in range(8):
        out_ref[n] = total


def subgrid_kernel(strip_ref, low_ref, high_ref, out_ref):
    low = strip_ref[:4].reshape(4 * STRIP, 2 * STRIP)
    high = strip_ref[4:].reshape(4 * STRIP, 2 * STRIP)
    for n in range(4):
        product = jnp.dot(low_ref[n], low, preferred_element_type=F32) + jnp.dot(
            high_ref[n], high, preferred_element_type=F32
        )
        out_ref[n, :STRIP] = (product[:STRIP, :STRIP] - product[STRIP:, STRIP:]).astype(BF16)
        out_ref[n, STRIP:] = (product[:STRIP, STRIP:] + product[STRIP:, :STRIP]).astype(BF16)


def place_kernel(place_ref, parts_ref, out_ref, scratch_ref):
    place = place_ref[0] & (SUBGRID - 1)
    scratch_ref[...] = jnp.zeros_like(scratch_ref)
    for part in range(2):
        rows = slice(STRIP * part, STRIP * (part + 1))
        total = parts_ref[0, rows, :].astype(F32)
        for n in range(1, 4):
            total += parts_ref[n, rows, :].astype(F32)
        scratch_ref[part, pl.ds(place, STRIP), :] = total
    out_ref[:, STRIP:, :] = scratch_ref[:, STRIP:SUBGRID, :]
    out_ref[:, :STRIP, :] = scratch_ref[:, :STRIP, :] + scratch_ref[:, SUBGRID:, :]


def call(kernel, specs, shape, dtype, scratch=(), flops=0, moved=1 << 20):
    return pl.pallas_call(
        kernel,
        out_shape=jax.ShapeDtypeStruct(shape, dtype),
        in_specs=specs,
        out_specs=VMEM,
        scratch_shapes=list(scratch),
        compiler_params=pltpu.CompilerParams(vmem_limit_bytes=24 * 1024 * 1024),
        cost_estimate=pl.CostEstimate(flops=flops, bytes_accessed=moved, transcendentals=0),
    )


def prepare(*operands):
    return pl.pallas_call(
        prepare_kernel,
        out_shape=(
            jax.ShapeDtypeStruct((2 * STRIP, HALF), BF16),
            jax.ShapeDtypeStruct((2 * STRIP + 16, HALF), F32),
        ),
        in_specs=[HBM] * 7,
        out_specs=(VMEM, VMEM),
        scratch_shapes=[
            pltpu.VMEM((2, HALF, STRIP), BF16),
            pltpu.VMEM((1, HALF), F32),
            pltpu.VMEM((32, STRIP), F32),
            pltpu.SMEM((16,), jnp.int32),
            pltpu.SMEM((32,), jnp.int32),
            pltpu.SMEM((16, 32), jnp.int32),
            pltpu.SemaphoreType.DMA((7,)),
        ],
        compiler_params=pltpu.CompilerParams(vmem_limit_bytes=60 * 1024 * 1024),
        cost_estimate=pl.CostEstimate(flops=0, bytes_accessed=1 << 20, transcendentals=0),
    )(*operands)


SPREAD = [[16 * xl + 4 * n + (s + n) % 4 for n in range(4)] for xl in range(2) for s in range(4)]


def on_device(
    facets, row_taper, column_taper, column_place, row_offset, column_offset, slot_subgrid
):
    turned_scratch = [pltpu.VMEM((2, STRIP, HALF), F32)]
    own, pack = prepare(
        facets,
        row_taper.reshape(1, HALF),
        column_taper.reshape(32, STRIP),
        row_offset,
        column_offset,
        slot_subgrid,
        jnp.asarray(base_table().reshape(2 * STRIP, HALF)),
    )
    other = lax.ppermute(own, "core", [(0, 1), (1, 0)])
    encode = call(
        encode_kernel, [VMEM], (8, 2 * STRIP, 2 * HALF), BF16, turned_scratch, moved=3 << 20
    )(pack)
    shares = call(strip_kernel, [VMEM] * 3, (8, STRIP, 2 * STRIP), BF16, flops=1 << 29)(
        own, other, encode
    )

    def decode(xl, pack):
        kernel = functools.partial(decode_kernel, xl)
        shape = (4, 2 * STRIP, 2 * HALF)
        return call(kernel, [VMEM], shape, BF16, turned_scratch, moved=2 << 20)(pack)

    shares, pack = lax.optimization_barrier((shares, pack))
    low = decode(0, pack)
    shares, low = lax.optimization_barrier((lax.all_to_all(shares, ("xh", "y"), 0, 0), low))
    strip = call(sum_kernel, [VMEM], (8, STRIP, 2 * STRIP), BF16)(shares)
    strip, pack = lax.optimization_barrier((strip, pack))
    high = decode(1, pack)
    strips = lax.all_to_all(strip, ("xl", "zl"), 0, 0)
    partial = call(subgrid_kernel, [VMEM] * 3, (4, 2 * STRIP, STRIP), BF16, flops=1 << 29)(
        strips, low, high
    )
    received = lax.all_to_all(partial, FAC, 0, 0, axis_index_groups=SPREAD)
    subgrid = call(
        place_kernel,
        [SMEM, VMEM],
        (2, SUBGRID, STRIP),
        F32,
        [pltpu.VMEM((2, SUBGRID + STRIP, STRIP), F32)],
    )(column_place, received)
    return subgrid.reshape(1, 1, 2, SUBGRID, STRIP)


def solution(mesh):
    split = Mesh(mesh.devices.reshape(SIZES), SPLIT)
    in_specs = (P(None, COL, FAC), P(COL), P(), P(), P(), P(), P())
    return jax.shard_map(
        on_device,
        mesh=split,
        in_specs=in_specs,
        out_specs=P(COL, FAC, None, None, None),
        check_vma=False,
    )
```

```python
import functools
import math

import jax
import jax.numpy as jnp
import numpy as np
from jax import lax
from jax.experimental import pallas as pl
from jax.experimental.pallas import tpu as pltpu
from jax.sharding import Mesh, PartitionSpec as P

FACET = 4096
STRIP = 128
SUBGRID = 512
HALF = 256
SPLIT = ("xh", "y", "core", "xl", "zh", "zl")
SIZES = (2, 4, 2, 2, 4, 4)
COL = SPLIT[:3]
FAC = SPLIT[3:]
F32 = jnp.float32
BF16 = jnp.bfloat16
VMEM = pl.BlockSpec(memory_space=pltpu.VMEM)
HBM = pl.BlockSpec(memory_space=pltpu.HBM)
SMEM = pl.BlockSpec(memory_space=pltpu.SMEM)
ENCODE = slice(2 * STRIP, 2 * STRIP + 8)
DECODE = slice(2 * STRIP + 8, 2 * STRIP + 16)
NT = (((1,), (1,)), ((), ()))


def base_table():
    k = np.arange(STRIP)[:, None]
    j = np.arange(HALF)[None, :]
    angle = (k * j % FACET) * (2.0 * math.pi / FACET)
    scale = 1.0 / math.sqrt(FACET)
    return np.stack([np.cos(angle) * scale, -np.sin(angle) * scale]).astype(np.float32)


def unit(phase):
    angle = phase.astype(F32) * (2.0 * math.pi / FACET)
    return jnp.cos(angle), -jnp.sin(angle)


def turned(pack_ref, turned_ref, block):
    k = lax.broadcasted_iota(jnp.int32, (16, HALF), 0)
    real, imag = unit((k * block & 15) * HALF)
    for row in range(0, STRIP, 16):
        rows = pl.ds(row, 16)
        base_real, base_imag = pack_ref[rows, :], pack_ref[pl.ds(STRIP + row, 16), :]
        turned_ref[0, rows, :] = base_real * real - base_imag * imag
        turned_ref[1, rows, :] = base_real * imag + base_imag * real


def position():
    core, xl, zh, zl = (lax.axis_index(name) for name in ("core", "xl", "zh", "zl"))
    place = (4 * zh + zl - 2 * core) & 15
    return core, xl, place >> 2, place & 3


def spread(starts):
    row = lax.broadcasted_iota(jnp.int32, (8, HALF), 0)
    first = jnp.zeros((8, HALF), jnp.int32)
    for n, start in enumerate(starts):
        first = jnp.where(row == n, start, first)
    return first.astype(F32)


def fill_tables(pack_ref, firsts, count, blocks, out_ref, turned_ref):
    lane = lax.broadcasted_iota(jnp.int32, (8, HALF), 1)
    first = pack_ref[firsts].astype(jnp.int32)
    for c, block in enumerate(blocks):
        turned(pack_ref, turned_ref, block)
        real, imag = unit(first * (block * HALF + lane) & (FACET - 1))
        for k in range(0, STRIP, 16):
            rows = pl.ds(k, 16)
            base_real, base_imag = turned_ref[0, rows, :], turned_ref[1, rows, :]
            for n in range(count):
                own_real, own_imag = real[n : n + 1], imag[n : n + 1]
                out_ref[n, rows, HALF * c : HALF * (c + 1)] = (
                    own_real * base_real - own_imag * base_imag
                ).astype(BF16)
                out_ref[n, pl.ds(STRIP + k, 16), HALF * c : HALF * (c + 1)] = (
                    own_real * base_imag + own_imag * base_real
                ).astype(BF16)


def prepare_kernel(
    facets_hbm,
    row_hbm,
    column_hbm,
    row_offset_hbm,
    offset_hbm,
    slot_hbm,
    base_hbm,
    out_hbm,
    pack_hbm,
    facets_ref,
    row_ref,
    column_ref,
    row_offset_ref,
    offset_ref,
    slot_ref,
    out_ref,
    pack_ref,
    sems,
    out_sems,
):
    core, xl, line, step = position()
    pair = lax.axis_index("xh") * 4 + lax.axis_index("y")
    fac = (xl * 4 + lax.axis_index("zh")) * 4 + lax.axis_index("zl")
    copies = [
        pltpu.make_async_copy(source, target, sems.at[n])
        for n, (source, target) in enumerate(
            [
                (facets_hbm, facets_ref),
                (row_hbm, row_ref),
                (column_hbm, column_ref),
                (row_offset_hbm, row_offset_ref),
                (offset_hbm, offset_ref),
                (slot_hbm, slot_ref),
                (base_hbm, pack_ref.at[pl.ds(0, 2 * STRIP)]),
            ]
        )
    ]
    for copy in copies:
        copy.start()
    for copy in copies[:3]:
        copy.wait()
    column = column_ref[pl.ds(fac, 1), :]
    for part in range(2):
        scaled = facets_ref[part].astype(F32) * column
        out_ref[STRIP * part : STRIP * (part + 1), :] = (scaled.T * row_ref[...]).astype(BF16)
    own_copy = pltpu.make_async_copy(out_ref, out_hbm, out_sems.at[0])
    own_copy.start()
    for copy in copies[3:6]:
        copy.wait()
    pack_ref[ENCODE] = spread([row_offset_ref[2 * n + core] for n in range(8)])
    pack_ref[DECODE] = spread(
        [
            offset_ref[
                slot_ref[
                    2 * pair + core, 16 * xl + ((4 * n + 2 * core + ((step - line + n) & 3)) & 15)
                ]
                & 31
            ]
            for n in range(4)
        ]
    )
    copies[6].wait()
    pack_copy = pltpu.make_async_copy(pack_ref, pack_hbm, out_sems.at[1])
    pack_copy.start()
    own_copy.wait()
    pack_copy.wait()


def encode_kernel(pack_ref, out_ref, turned_ref):
    core = lax.axis_index("core")
    pair = lax.axis_index("xh") * 4 + lax.axis_index("y")
    fill_tables(pack_ref, ENCODE, 8, [2 * pair + core, 2 * pair + 1 - core], out_ref, turned_ref)


def decode_kernel(xl, pack_ref, out_ref, turned_ref):
    core, _, line, _ = position()
    blocks = [8 * xl + ((2 * line + core + half) & 7) for half in range(2)]
    fill_tables(pack_ref, DECODE, 4, blocks, out_ref, turned_ref)


def sent(n, out_ref, out_hbm, sems):
    copy = pltpu.make_async_copy(out_ref.at[n], out_hbm.at[n], sems.at[n])
    copy.start()
    return copy


def strip_kernel(own_ref, other_ref, table_ref, out_hbm, out_ref, sems):
    copies = []
    for n in range(8):
        product = lax.dot_general(
            own_ref[...], table_ref[n, :, :HALF], NT, preferred_element_type=F32
        ) + lax.dot_general(
            other_ref[...], table_ref[n, :, HALF:], NT, preferred_element_type=F32
        )
        out_ref[n, :, :STRIP] = (product[:STRIP, :STRIP] - product[STRIP:, STRIP:]).astype(BF16)
        out_ref[n, :, STRIP:] = (product[:STRIP, STRIP:] + product[STRIP:, :STRIP]).astype(BF16)
        copies.append(sent(n, out_ref, out_hbm, sems))
    for copy in copies:
        copy.wait()


def sum_kernel(parts_ref, out_hbm, total_ref, sems):
    total = parts_ref[0].astype(F32)
    for n in range(1, 8):
        total += parts_ref[n].astype(F32)
    total_ref[...] = total.astype(BF16)
    copies = [pltpu.make_async_copy(total_ref, out_hbm.at[n], sems.at[n]) for n in range(8)]
    for copy in copies:
        copy.start()
    for copy in copies:
        copy.wait()


def subgrid_kernel(strip_ref, low_ref, high_ref, out_hbm, out_ref, sems):
    low = strip_ref[:4].reshape(4 * STRIP, 2 * STRIP)
    high = strip_ref[4:].reshape(4 * STRIP, 2 * STRIP)
    copies = []
    for n in range(4):
        product = jnp.dot(low_ref[n], low, preferred_element_type=F32) + jnp.dot(
            high_ref[n], high, preferred_element_type=F32
        )
        out_ref[n, :STRIP] = (product[:STRIP, :STRIP] - product[STRIP:, STRIP:]).astype(BF16)
        out_ref[n, STRIP:] = (product[:STRIP, STRIP:] + product[STRIP:, :STRIP]).astype(BF16)
        copies.append(sent(n, out_ref, out_hbm, sems))
    for copy in copies:
        copy.wait()


def place_kernel(place_ref, parts_ref, out_hbm, scratch_ref, sems):
    place = place_ref[0] & (SUBGRID - 1)
    scratch_ref[...] = jnp.zeros_like(scratch_ref)
    copies = []
    for part in range(2):
        rows = slice(STRIP * part, STRIP * (part + 1))
        total = parts_ref[0, rows, :].astype(F32)
        for n in range(1, 4):
            total += parts_ref[n, rows, :].astype(F32)
        scratch_ref[part, pl.ds(place, STRIP), :] = total
        scratch_ref[part, :STRIP, :] += scratch_ref[part, SUBGRID:, :]
        copy = pltpu.make_async_copy(
            scratch_ref.at[part, pl.ds(0, SUBGRID)], out_hbm.at[part], sems.at[part]
        )
        copy.start()
        copies.append(copy)
    for copy in copies:
        copy.wait()


def call(kernel, specs, shape, dtype, scratch=(), flops=0, moved=1 << 20, out=VMEM):
    return pl.pallas_call(
        kernel,
        out_shape=jax.ShapeDtypeStruct(shape, dtype),
        in_specs=specs,
        out_specs=out,
        scratch_shapes=list(scratch),
        compiler_params=pltpu.CompilerParams(vmem_limit_bytes=24 * 1024 * 1024),
        cost_estimate=pl.CostEstimate(flops=flops, bytes_accessed=moved, transcendentals=0),
    )


def prepare(*operands):
    return pl.pallas_call(
        prepare_kernel,
        out_shape=(
            jax.ShapeDtypeStruct((2 * STRIP, HALF), BF16),
            jax.ShapeDtypeStruct((2 * STRIP + 16, HALF), F32),
        ),
        in_specs=[HBM] * 7,
        out_specs=(HBM, HBM),
        scratch_shapes=[
            pltpu.VMEM((2, HALF, STRIP), BF16),
            pltpu.VMEM((1, HALF), F32),
            pltpu.VMEM((32, STRIP), F32),
            pltpu.SMEM((16,), jnp.int32),
            pltpu.SMEM((32,), jnp.int32),
            pltpu.SMEM((16, 32), jnp.int32),
            pltpu.VMEM((2 * STRIP, HALF), BF16),
            pltpu.VMEM((2 * STRIP + 16, HALF), F32),
            pltpu.SemaphoreType.DMA((7,)),
            pltpu.SemaphoreType.DMA((2,)),
        ],
        compiler_params=pltpu.CompilerParams(vmem_limit_bytes=60 * 1024 * 1024),
        cost_estimate=pl.CostEstimate(flops=0, bytes_accessed=1 << 20, transcendentals=0),
    )(*operands)


def groups():
    gather = [
        [32 * core + 16 * xl + (4 * n + 2 * core + j) % 16 for xl in range(2) for j in range(4)]
        for core in range(2)
        for n in range(4)
    ]
    reduce = [
        [32 * core + 16 * xl + (4 * n + 2 * core + (s + n) % 4) % 16 for n in range(4)]
        for core in range(2)
        for xl in range(2)
        for s in range(4)
    ]
    return gather, reduce


def on_device(
    facets, row_taper, column_taper, column_place, row_offset, column_offset, slot_subgrid
):
    turned_scratch = [pltpu.VMEM((2, STRIP, HALF), F32)]
    own, pack = prepare(
        facets,
        row_taper.reshape(1, HALF),
        column_taper.reshape(32, STRIP),
        row_offset,
        column_offset,
        slot_subgrid,
        jnp.asarray(base_table().reshape(2 * STRIP, HALF)),
    )
    other = lax.ppermute(own, "core", [(0, 1), (1, 0)])
    encode = call(
        encode_kernel, [VMEM], (8, 2 * STRIP, 2 * HALF), BF16, turned_scratch, moved=3 << 20
    )(pack)
    blocks = (8, STRIP, 2 * STRIP)
    eight = pltpu.SemaphoreType.DMA((8,))
    shares = call(
        strip_kernel,
        [VMEM] * 3,
        blocks,
        BF16,
        [pltpu.VMEM(blocks, BF16), eight],
        flops=1 << 29,
        out=HBM,
    )(own, other, encode)

    def decode(xl, pack):
        kernel = functools.partial(decode_kernel, xl)
        shape = (4, 2 * STRIP, 2 * HALF)
        return call(kernel, [VMEM], shape, BF16, turned_scratch, moved=2 << 20)(pack)

    gather, reduce = groups()
    line = ("core",) + FAC
    shares, pack = lax.optimization_barrier((shares, pack))
    low = decode(0, pack)
    shares, low = lax.optimization_barrier((lax.all_to_all(shares, ("xh", "y"), 0, 0), low))
    strip = call(
        sum_kernel, [VMEM], blocks, BF16, [pltpu.VMEM(blocks[1:], BF16), eight], out=HBM
    )(shares)
    strip, pack = lax.optimization_barrier((strip, pack))
    high = decode(1, pack)
    strips = lax.all_to_all(strip, line, 0, 0, axis_index_groups=gather)
    quarters = (4, 2 * STRIP, STRIP)
    partial = call(
        subgrid_kernel,
        [VMEM] * 3,
        quarters,
        BF16,
        [pltpu.VMEM(quarters, BF16), pltpu.SemaphoreType.DMA((4,))],
        flops=1 << 29,
        out=HBM,
    )(strips, low, high)
    received = lax.all_to_all(partial, line, 0, 0, axis_index_groups=reduce)
    subgrid = call(
        place_kernel,
        [SMEM, VMEM],
        (2, SUBGRID, STRIP),
        F32,
        [pltpu.VMEM((2, SUBGRID + STRIP, STRIP), F32), pltpu.SemaphoreType.DMA((2,))],
        out=HBM,
    )(column_place, received)
    return subgrid.reshape(1, 1, 2, SUBGRID, STRIP)


def solution(mesh):
    split = Mesh(mesh.devices.reshape(SIZES), SPLIT)
    in_specs = (P(None, COL, FAC), P(COL), P(), P(), P(), P(), P())
    return jax.shard_map(
        on_device,
        mesh=split,
        in_specs=in_specs,
        out_specs=P(COL, FAC, None, None, None),
        check_vma=False,
    )
```

```python
import math

import jax
import jax.numpy as jnp
import numpy as np
from jax import lax
from jax.experimental import pallas as pl
from jax.experimental.pallas import tpu as pltpu
from jax.sharding import Mesh, PartitionSpec as P

FACET = 4096
STRIP = 128
SUBGRID = 512
HALF = 256
SPLIT = ("xh", "y", "core", "xl", "zh", "zl")
SIZES = (2, 4, 2, 2, 4, 4)
COL = SPLIT[:3]
FAC = SPLIT[3:]
PLANE = (0, 1, 2, 3, 4, 5, 6, 7)
RUN = (0, 1, 2, 3, 4, 5, 6, 7)
RUNS = ((3, 2, 1, 0), (3, 2, 1, 0))
TWIST = (0, 1, 2, 3)
F32 = jnp.float32
BF16 = jnp.bfloat16
VMEM = pl.BlockSpec(memory_space=pltpu.VMEM)
HBM = pl.BlockSpec(memory_space=pltpu.HBM)
SMEM = pl.BlockSpec(memory_space=pltpu.SMEM)
ENCODE = slice(2 * STRIP, 2 * STRIP + 8)
DECODE = slice(2 * STRIP + 8, 2 * STRIP + 16)
NT = (((1,), (1,)), ((), ()))


def base_table():
    k = np.arange(STRIP)[:, None]
    j = np.arange(HALF)[None, :]
    angle = (k * j % FACET) * (2.0 * math.pi / FACET)
    scale = 1.0 / math.sqrt(FACET)
    return np.stack([np.cos(angle) * scale, -np.sin(angle) * scale]).astype(np.float32)


def unit(phase):
    angle = phase.astype(F32) * (2.0 * math.pi / FACET)
    return jnp.cos(angle), -jnp.sin(angle)


def turned(pack_ref, turned_ref, block):
    k = lax.broadcasted_iota(jnp.int32, (16, HALF), 0)
    real, imag = unit((k * block & 15) * HALF)
    for row in range(0, STRIP, 16):
        rows = pl.ds(row, 16)
        base_real, base_imag = pack_ref[rows, :], pack_ref[pl.ds(STRIP + row, 16), :]
        turned_ref[0, rows, :] = base_real * real - base_imag * imag
        turned_ref[1, rows, :] = base_real * imag + base_imag * real


def position():
    core, xl, zh, zl = (lax.axis_index(name) for name in ("core", "xl", "zh", "zl"))
    place = (4 * zh + zl - 2 * core) & 15
    return core, xl, place >> 2, place & 3


def spread(starts):
    row = lax.broadcasted_iota(jnp.int32, (8, HALF), 0)
    first = jnp.zeros((8, HALF), jnp.int32)
    for n, start in enumerate(starts):
        first = jnp.where(row == n, start, first)
    return first.astype(F32)


def fill_tables(pack_ref, firsts, count, blocks, out_ref, turned_ref):
    lane = lax.broadcasted_iota(jnp.int32, (8, HALF), 1)
    first = pack_ref[firsts].astype(jnp.int32)
    for c, block in enumerate(blocks):
        turned(pack_ref, turned_ref, block)
        real, imag = unit(first * (block * HALF + lane) & (FACET - 1))
        for k in range(0, STRIP, 16):
            rows = pl.ds(k, 16)
            base_real, base_imag = turned_ref[0, rows, :], turned_ref[1, rows, :]
            for n in range(count):
                own_real, own_imag = real[n : n + 1], imag[n : n + 1]
                out_ref[n, rows, HALF * c : HALF * (c + 1)] = (
                    own_real * base_real - own_imag * base_imag
                ).astype(BF16)
                out_ref[n, pl.ds(STRIP + k, 16), HALF * c : HALF * (c + 1)] = (
                    own_real * base_imag + own_imag * base_real
                ).astype(BF16)


def prepare_kernel(
    facets_hbm,
    row_hbm,
    column_hbm,
    row_offset_hbm,
    offset_hbm,
    slot_hbm,
    base_hbm,
    out_hbm,
    pack_hbm,
    facets_ref,
    row_ref,
    column_ref,
    row_offset_ref,
    offset_ref,
    slot_ref,
    out_ref,
    pack_ref,
    sems,
    out_sems,
):
    core, xl, line, step = position()
    pair = lax.axis_index("xh") * 4 + lax.axis_index("y")
    fac = (xl * 4 + lax.axis_index("zh")) * 4 + lax.axis_index("zl")
    copies = [
        pltpu.make_async_copy(source, target, sems.at[n])
        for n, (source, target) in enumerate(
            [
                (facets_hbm, facets_ref),
                (row_hbm, row_ref),
                (column_hbm, column_ref),
                (row_offset_hbm, row_offset_ref),
                (offset_hbm, offset_ref),
                (slot_hbm, slot_ref),
                (base_hbm, pack_ref.at[pl.ds(0, 2 * STRIP)]),
            ]
        )
    ]
    for copy in copies:
        copy.start()
    for copy in copies[:3]:
        copy.wait()
    column = column_ref[pl.ds(fac, 1), :]
    for part in range(2):
        scaled = facets_ref[part].astype(F32) * column
        out_ref[STRIP * part : STRIP * (part + 1), :] = (scaled.T * row_ref[...]).astype(BF16)
    own_copy = pltpu.make_async_copy(out_ref, out_hbm, out_sems.at[0])
    own_copy.start()
    for copy in copies[3:6]:
        copy.wait()
    pack_ref[ENCODE] = spread([row_offset_ref[2 * n + core] for n in PLANE])
    slots = []
    twist = sum(jnp.where(line == n, TWIST[n], 0) for n in range(4))
    for first, second in zip(*RUNS):
        run = jnp.where(core == 0, first, second)
        away = jnp.where(core == 0, TWIST[first], TWIST[second])
        slots.append(16 * xl + ((4 * run + 2 * core + ((step - twist + away) & 3)) & 15))
    pack_ref[DECODE] = spread([offset_ref[slot_ref[2 * pair + core, slot] & 31] for slot in slots])
    copies[6].wait()
    pack_copy = pltpu.make_async_copy(pack_ref, pack_hbm, out_sems.at[1])
    pack_copy.start()
    own_copy.wait()
    pack_copy.wait()


def encode_kernel(pack_ref, out_ref, turned_ref):
    core = lax.axis_index("core")
    pair = lax.axis_index("xh") * 4 + lax.axis_index("y")
    fill_tables(pack_ref, ENCODE, 8, [2 * pair + core, 2 * pair + 1 - core], out_ref, turned_ref)


def decode_kernel(place_ref, pack_ref, out_ref, spot_ref, turned_ref):
    spot_ref[...] = jnp.full((8, STRIP), place_ref[0], jnp.int32)
    core, _, line, _ = position()
    blocks = [8 * xl + ((2 * line + core + half) & 7) for xl in range(2) for half in range(2)]
    fill_tables(pack_ref, DECODE, 4, blocks, out_ref, turned_ref)


def strip_kernel(own_ref, other_ref, table_ref, out_ref):
    for n in range(8):
        product = lax.dot_general(
            own_ref[...], table_ref[n, :, :HALF], NT, preferred_element_type=F32
        ) + lax.dot_general(
            other_ref[...], table_ref[n, :, HALF:], NT, preferred_element_type=F32
        )
        out_ref[n, :, :STRIP] = (product[:STRIP, :STRIP] - product[STRIP:, STRIP:]).astype(BF16)
        out_ref[n, :, STRIP:] = (product[:STRIP, STRIP:] + product[STRIP:, :STRIP]).astype(BF16)


def sum_kernel(parts_ref, out_hbm, total_ref, sems):
    total = parts_ref[0].astype(F32)
    for n in range(1, 8):
        total += parts_ref[n].astype(F32)
    total_ref[...] = total.astype(BF16)
    copies = [pltpu.make_async_copy(total_ref, out_hbm.at[n], sems.at[n]) for n in range(8)]
    for copy in copies:
        copy.start()
    for copy in copies:
        copy.wait()


def subgrid_kernel(strip_ref, table_ref, out_ref):
    strip = jnp.concatenate([strip_ref[RUN.index(n)] for n in range(8)])
    for n in range(4):
        product = jnp.dot(table_ref[n], strip, preferred_element_type=F32)
        out_ref[n, :STRIP] = (product[:STRIP, :STRIP] - product[STRIP:, STRIP:]).astype(BF16)
        out_ref[n, STRIP:] = (product[:STRIP, STRIP:] + product[STRIP:, :STRIP]).astype(BF16)


def place_kernel(place_ref, parts_ref, out_hbm, scratch_ref, sems):
    place = jnp.max(place_ref[...]) & (SUBGRID - 1)
    scratch_ref[...] = jnp.zeros_like(scratch_ref)
    copies = []
    for part in range(2):
        rows = slice(STRIP * part, STRIP * (part + 1))
        total = parts_ref[0, rows, :].astype(F32)
        for n in range(1, 4):
            total += parts_ref[n, rows, :].astype(F32)
        scratch_ref[part, pl.ds(place, STRIP), :] = total
        scratch_ref[part, :STRIP, :] += scratch_ref[part, SUBGRID:, :]
        copy = pltpu.make_async_copy(
            scratch_ref.at[part, pl.ds(0, SUBGRID)], out_hbm.at[part], sems.at[part]
        )
        copy.start()
        copies.append(copy)
    for copy in copies:
        copy.wait()


def call(kernel, specs, shape, dtype, scratch=(), flops=0, moved=1 << 20, out=VMEM):
    if isinstance(shape, list):
        result = [jax.ShapeDtypeStruct(*pair) for pair in zip(shape, dtype)]
    else:
        result = jax.ShapeDtypeStruct(shape, dtype)
    return pl.pallas_call(
        kernel,
        out_shape=result,
        in_specs=specs,
        out_specs=out,
        scratch_shapes=list(scratch),
        compiler_params=pltpu.CompilerParams(vmem_limit_bytes=24 * 1024 * 1024),
        cost_estimate=pl.CostEstimate(flops=flops, bytes_accessed=moved, transcendentals=0),
    )


def prepare(*operands):
    return pl.pallas_call(
        prepare_kernel,
        out_shape=(
            jax.ShapeDtypeStruct((2 * STRIP, HALF), BF16),
            jax.ShapeDtypeStruct((2 * STRIP + 16, HALF), F32),
        ),
        in_specs=[HBM] * 7,
        out_specs=(HBM, HBM),
        scratch_shapes=[
            pltpu.VMEM((2, HALF, STRIP), BF16),
            pltpu.VMEM((1, HALF), F32),
            pltpu.VMEM((32, STRIP), F32),
            pltpu.SMEM((16,), jnp.int32),
            pltpu.SMEM((32,), jnp.int32),
            pltpu.SMEM((16, 32), jnp.int32),
            pltpu.VMEM((2 * STRIP, HALF), BF16),
            pltpu.VMEM((2 * STRIP + 16, HALF), F32),
            pltpu.SemaphoreType.DMA((7,)),
            pltpu.SemaphoreType.DMA((2,)),
        ],
        compiler_params=pltpu.CompilerParams(vmem_limit_bytes=60 * 1024 * 1024),
        cost_estimate=pl.CostEstimate(flops=0, bytes_accessed=1 << 20, transcendentals=0),
    )(*operands)


def groups():
    gather = [
        [32 * core + 16 * (j // 4) + (4 * n + 2 * core + j % 4) % 16 for j in RUN]
        for core in range(2)
        for n in range(4)
    ]
    reduce = [
        [32 * core + 16 * xl + (4 * n + 2 * core + (s + TWIST[n]) % 4) % 16 for n in RUNS[core]]
        for core in range(2)
        for xl in range(2)
        for s in range(4)
    ]
    return gather, reduce


def on_device(
    facets, row_taper, column_taper, column_place, row_offset, column_offset, slot_subgrid
):
    turned_scratch = [pltpu.VMEM((2, STRIP, HALF), F32)]
    own, pack = prepare(
        facets,
        row_taper.reshape(1, HALF),
        column_taper.reshape(32, STRIP),
        row_offset,
        column_offset,
        slot_subgrid,
        jnp.asarray(base_table().reshape(2 * STRIP, HALF)),
    )
    other = lax.ppermute(own, "core", [(0, 1), (1, 0)])
    encode = call(
        encode_kernel, [VMEM], (8, 2 * STRIP, 2 * HALF), BF16, turned_scratch, moved=3 << 20
    )(pack)
    blocks = (8, STRIP, 2 * STRIP)
    shares = call(strip_kernel, [VMEM] * 3, blocks, BF16, flops=1 << 29)(own, other, encode)
    gather, reduce = groups()
    line = ("core",) + FAC
    shares = lax.all_to_all(shares, ("xh", "y"), 0, 0, axis_index_groups=[list(PLANE)])
    strip = call(
        sum_kernel,
        [VMEM],
        blocks,
        BF16,
        [pltpu.VMEM(blocks[1:], BF16), pltpu.SemaphoreType.DMA((8,))],
        out=HBM,
    )(shares)
    strip, pack = lax.optimization_barrier((strip, pack))
    decode, spot = call(
        decode_kernel,
        [SMEM, VMEM],
        [(4, 2 * STRIP, 4 * HALF), (8, STRIP)],
        [BF16, jnp.int32],
        turned_scratch,
        moved=3 << 20,
        out=[VMEM, VMEM],
    )(column_place, pack)
    strips = lax.all_to_all(strip, line, 0, 0, axis_index_groups=gather)
    quarters = (4, 2 * STRIP, STRIP)
    partial = call(
        subgrid_kernel,
        [VMEM] * 2,
        quarters,
        BF16,
        flops=1 << 29,
    )(strips, decode)
    received = lax.all_to_all(partial, line, 0, 0, axis_index_groups=reduce)
    subgrid = call(
        place_kernel,
        [VMEM, VMEM],
        (2, SUBGRID, STRIP),
        F32,
        [pltpu.VMEM((2, SUBGRID + STRIP, STRIP), F32), pltpu.SemaphoreType.DMA((2,))],
        out=HBM,
    )(spot, received)
    return subgrid.reshape(1, 1, 2, SUBGRID, STRIP)


def solution(mesh):
    split = Mesh(mesh.devices.reshape(SIZES), SPLIT)
    in_specs = (P(None, COL, FAC), P(COL), P(), P(), P(), P(), P())
    return jax.shard_map(
        on_device,
        mesh=split,
        in_specs=in_specs,
        out_specs=P(COL, FAC, None, None, None),
        check_vma=False,
    )
```

```python
import math

import jax
import jax.numpy as jnp
import numpy as np
from jax import lax
from jax.experimental import pallas as pl
from jax.experimental.pallas import tpu as pltpu
from jax.sharding import Mesh, PartitionSpec as P

FACET = 4096
STRIP = 128
SUBGRID = 512
HALF = 256
SPLIT = ("xh", "y", "core", "xl", "zh", "zl")
SIZES = (2, 4, 2, 2, 4, 4)
COL = SPLIT[:3]
FAC = SPLIT[3:]
RUN = (0, 1, 2, 3)
RUNS = ((3, 2, 1, 0), (3, 2, 1, 0))
TWIST = (0, 1, 2, 3)
F32 = jnp.float32
BF16 = jnp.bfloat16
VMEM = pl.BlockSpec(memory_space=pltpu.VMEM)
HBM = pl.BlockSpec(memory_space=pltpu.HBM)
SMEM = pl.BlockSpec(memory_space=pltpu.SMEM)
BASE = 48
ENCODE = slice(BASE, BASE + 8)
DECODE = slice(BASE + 8, BASE + 16)
OWN = slice(BASE + 16, BASE + 16 + HALF)
AHEAD = 6
NT = (((1,), (1,)), ((), ()))


def base_table():
    def rows(ks, scale):
        angle = (ks[:, None] * np.arange(HALF)[None, :] % FACET) * (2.0 * math.pi / FACET)
        return [np.cos(angle) * scale, -np.sin(angle) * scale]

    small, large = np.arange(16), 16 * np.arange(8)
    return np.concatenate(rows(small, 1.0) + rows(large, 1.0 / math.sqrt(FACET))).astype(np.float32)


def unit(phase):
    angle = phase.astype(F32) * (2.0 * math.pi / FACET)
    return jnp.cos(angle), -jnp.sin(angle)


def turned(pack_ref, turned_ref, block):
    k = lax.broadcasted_iota(jnp.int32, (16, HALF), 0)
    real, imag = unit((k * block & 15) * HALF)
    base_real, base_imag = pack_ref[0:16, :], pack_ref[16:32, :]
    real, imag = base_real * real - base_imag * imag, base_real * imag + base_imag * real
    for large in range(8):
        row_real = pack_ref[32 + large : 33 + large, :]
        row_imag = pack_ref[40 + large : 41 + large, :]
        rows = pl.ds(16 * large, 16)
        turned_ref[0, rows, :] = row_real * real - row_imag * imag
        turned_ref[1, rows, :] = row_real * imag + row_imag * real


def position():
    core, xl, zh, zl = (lax.axis_index(name) for name in ("core", "xl", "zh", "zl"))
    place = (4 * zh + zl - 2 * core) & 15
    return core, xl, place >> 2, place & 3


def spread(starts):
    row = lax.broadcasted_iota(jnp.int32, (8, HALF), 0)
    first = jnp.zeros((8, HALF), jnp.int32)
    for n, start in enumerate(starts):
        first = jnp.where(row == n, start, first)
    return first.astype(F32)


def fill_tables(pack_ref, firsts, turn, blocks, outs, turned_ref):
    lane = lax.broadcasted_iota(jnp.int32, (8, HALF), 1)
    first = pack_ref[firsts].astype(jnp.int32)
    for c, block in enumerate(blocks):
        turned(pack_ref, turned_ref, block)
        real, imag = unit(first * (block * HALF + lane) & (FACET - 1))
        for k in range(0, STRIP, 16):
            rows = pl.ds(k, 16)
            base_real, base_imag = turned_ref[0, rows, :], turned_ref[1, rows, :]
            row = k // turn * 2 * turn + k % turn
            for n, out in outs.items():
                own_real, own_imag = real[n : n + 1], imag[n : n + 1]
                out[pl.ds(row, 16), HALF * c : HALF * (c + 1)] = (
                    own_real * base_real - own_imag * base_imag
                ).astype(BF16)
                out[pl.ds(row + turn, 16), HALF * c : HALF * (c + 1)] = (
                    own_real * base_imag + own_imag * base_real
                ).astype(BF16)


def prepare_kernel(
    facets_hbm,
    row_hbm,
    column_hbm,
    row_offset_hbm,
    offset_hbm,
    slot_hbm,
    base_hbm,
    out_hbm,
    first_hbm,
    pack_hbm,
    facets_ref,
    row_ref,
    column_ref,
    row_offset_ref,
    offset_ref,
    slot_ref,
    out_ref,
    pack_ref,
    sems,
    out_sems,
):
    core, xl, line, step = position()
    pair = lax.axis_index("xh") * 4 + lax.axis_index("y")
    fac = (xl * 4 + lax.axis_index("zh")) * 4 + lax.axis_index("zl")
    copies = [
        pltpu.make_async_copy(source, target, sems.at[n])
        for n, (source, target) in enumerate(
            [
                (facets_hbm, facets_ref),
                (row_hbm, row_ref),
                (column_hbm, column_ref),
                (row_offset_hbm, row_offset_ref),
                (offset_hbm, offset_ref),
                (slot_hbm, slot_ref),
                (base_hbm, pack_ref.at[pl.ds(0, BASE)]),
            ]
        )
    ]
    for copy in copies:
        copy.start()
    for copy in copies[:3]:
        copy.wait()
    column = column_ref[pl.ds(fac, 1), :]
    for part in range(2):
        scaled = facets_ref[part].astype(F32) * column
        block = (scaled.T * row_ref[...]).astype(BF16)
        out_ref[STRIP * part : STRIP * (part + 1), :] = block
        pack_ref[BASE + 16 + STRIP * part : BASE + 16 + STRIP * (part + 1), :] = block.astype(F32)
    own_copy = pltpu.make_async_copy(out_ref, out_hbm, out_sems.at[0])
    own_copy.start()
    for copy in copies[3:6]:
        copy.wait()
    pack_ref[ENCODE] = spread([row_offset_ref[2 * n + core] for n in range(8)])
    slots = []
    twist = sum(jnp.where(line == n, TWIST[n], 0) for n in range(4))
    for first, second in zip(*RUNS):
        run = jnp.where(core == 0, first, second)
        away = jnp.where(core == 0, TWIST[first], TWIST[second])
        slots.append((4 * run + 2 * core + ((step - twist + away) & 3)) & 15)
    slots += [slot + 16 for slot in slots]
    pack_ref[DECODE] = spread([offset_ref[slot_ref[2 * pair + core, slot] & 31] for slot in slots])
    copies[6].wait()
    first_copy = pltpu.make_async_copy(pack_ref, first_hbm, out_sems.at[1])
    first_copy.start()
    pack_copy = pltpu.make_async_copy(pack_ref.at[pl.ds(0, BASE + 16)], pack_hbm, out_sems.at[2])
    pack_copy.start()
    own_copy.wait()
    first_copy.wait()
    pack_copy.wait()


def encode_kernel(pack_ref, out_ref, turned_ref):
    core = lax.axis_index("core")
    pair = lax.axis_index("xh") * 4 + lax.axis_index("y")
    outs = {n: out_ref.at[n] for n in range(8)}
    blocks = [2 * pair + core, 2 * pair + 1 - core]
    fill_tables(pack_ref, ENCODE, STRIP // 2, blocks, outs, turned_ref)


def decode_tables(pack_ref, outs, turned_ref):
    core, _, line, _ = position()
    blocks = [8 * xl + ((2 * line + core + half) & 7) for xl in range(2) for half in range(2)]
    fill_tables(pack_ref, DECODE, STRIP, blocks, outs, turned_ref)


def decode_kernel(place_ref, pack_ref, out_ref, spot_ref, turned_ref):
    spot_ref[...] = jnp.full((8, STRIP), place_ref[0], jnp.int32)
    decode_tables(pack_ref, {n: out_ref.at[n] for n in range(AHEAD)}, turned_ref)


def joined(real_rows, imag_rows):
    lane = lax.broadcasted_iota(jnp.int32, real_rows.shape, 1)
    turned = pltpu.roll(imag_rows, STRIP // 2, 1)
    return real_rows + jnp.where(lane < STRIP // 2, -turned, turned)


def strip_kernel(first_ref, other_ref, table_ref, out_ref):
    own = first_ref[OWN].astype(BF16)
    for n in range(8):
        product = lax.dot_general(
            own, table_ref[n, :, :HALF], NT, preferred_element_type=F32
        ) + lax.dot_general(
            other_ref[...], table_ref[n, :, HALF:], NT, preferred_element_type=F32
        )
        for half in range(2):
            part = product[:, STRIP * half : STRIP * (half + 1)]
            out_ref[2 * n + half] = joined(part[:STRIP], part[STRIP:]).astype(BF16)


def sum_kernel(parts_ref, out_hbm, total_ref, sems):
    for xl in range(2):
        total = parts_ref[xl].astype(F32)
        for n in range(1, 8):
            total += parts_ref[2 * n + xl].astype(F32)
        total_ref[STRIP * xl : STRIP * (xl + 1), :] = total.astype(BF16)
    copies = [pltpu.make_async_copy(total_ref, out_hbm.at[n], sems.at[n]) for n in range(4)]
    for copy in copies:
        copy.start()
    for copy in copies:
        copy.wait()


def subgrid_kernel(strip_ref, ahead_ref, pack_ref, out_ref, late_ref, turned_ref):
    decode_tables(pack_ref, {n: late_ref.at[n - AHEAD] for n in range(AHEAD, 8)}, turned_ref)
    strip = jnp.concatenate(
        [
            strip_ref[RUN.index(n), STRIP * xl : STRIP * (xl + 1), :]
            for xl in range(2)
            for n in range(4)
        ]
    )
    for n in range(8):
        table = ahead_ref[n] if n < AHEAD else late_ref[n - AHEAD]
        product = jnp.dot(table, strip, preferred_element_type=F32)
        out_ref[n] = joined(product[:STRIP], product[STRIP:]).astype(BF16)


def place_kernel(place_ref, parts_ref, out_hbm, scratch_ref, sems):
    place = jnp.max(place_ref[...]) & (SUBGRID - 1)
    scratch_ref[...] = jnp.zeros_like(scratch_ref)
    halves = []
    for xl in range(2):
        total = parts_ref[4 * xl].astype(F32)
        for n in range(1, 4):
            total += parts_ref[4 * xl + n].astype(F32)
        halves.append(total)
    low = lax.broadcasted_iota(jnp.int32, (STRIP, STRIP), 1) < STRIP // 2
    copies = []
    for part in range(2):
        turned = pltpu.roll(halves[1 - part], STRIP // 2, 1)
        whole = jnp.where(low, turned, halves[1]) if part else jnp.where(low, halves[0], turned)
        scratch_ref[part, pl.ds(place, STRIP), :] = whole
        scratch_ref[part, :STRIP, :] += scratch_ref[part, SUBGRID:, :]
        copy = pltpu.make_async_copy(
            scratch_ref.at[part, pl.ds(0, SUBGRID)], out_hbm.at[part], sems.at[part]
        )
        copy.start()
        copies.append(copy)
    for copy in copies:
        copy.wait()


def call(kernel, specs, shape, dtype, scratch=(), flops=0, moved=1 << 20, out=VMEM):
    if isinstance(shape, list):
        result = [jax.ShapeDtypeStruct(*pair) for pair in zip(shape, dtype)]
    else:
        result = jax.ShapeDtypeStruct(shape, dtype)
    return pl.pallas_call(
        kernel,
        out_shape=result,
        in_specs=specs,
        out_specs=out,
        scratch_shapes=list(scratch),
        compiler_params=pltpu.CompilerParams(vmem_limit_bytes=24 * 1024 * 1024),
        cost_estimate=pl.CostEstimate(flops=flops, bytes_accessed=moved, transcendentals=0),
    )


def prepare(*operands):
    return pl.pallas_call(
        prepare_kernel,
        out_shape=(
            jax.ShapeDtypeStruct((2 * STRIP, HALF), BF16),
            jax.ShapeDtypeStruct((BASE + 16 + HALF, HALF), F32),
            jax.ShapeDtypeStruct((BASE + 16, HALF), F32),
        ),
        in_specs=[HBM] * 7,
        out_specs=(HBM, HBM, HBM),
        scratch_shapes=[
            pltpu.VMEM((2, HALF, STRIP), BF16),
            pltpu.VMEM((1, HALF), F32),
            pltpu.VMEM((32, STRIP), F32),
            pltpu.SMEM((16,), jnp.int32),
            pltpu.SMEM((32,), jnp.int32),
            pltpu.SMEM((16, 32), jnp.int32),
            pltpu.VMEM((2 * STRIP, HALF), BF16),
            pltpu.VMEM((BASE + 16 + HALF, HALF), F32),
            pltpu.SemaphoreType.DMA((7,)),
            pltpu.SemaphoreType.DMA((3,)),
        ],
        compiler_params=pltpu.CompilerParams(vmem_limit_bytes=60 * 1024 * 1024),
        cost_estimate=pl.CostEstimate(flops=0, bytes_accessed=1 << 20, transcendentals=0),
    )(*operands)


def groups():
    gather = [
        [32 * core + 16 * xl + (4 * n + 2 * core + j) % 16 for j in RUN]
        for core in range(2)
        for xl in range(2)
        for n in range(4)
    ]
    reduce = [
        [
            32 * core + 16 * xl + (4 * n + 2 * core + (s + TWIST[n]) % 4) % 16
            for xl in range(2)
            for n in RUNS[core]
        ]
        for core in range(2)
        for s in range(4)
    ]
    return gather, reduce


def on_device(
    facets, row_taper, column_taper, column_place, row_offset, column_offset, slot_subgrid
):
    turned_scratch = [pltpu.VMEM((2, STRIP, HALF), F32)]
    own, first, pack = prepare(
        facets,
        row_taper.reshape(1, HALF),
        column_taper.reshape(32, STRIP),
        row_offset,
        column_offset,
        slot_subgrid,
        jnp.asarray(base_table()),
    )
    other = lax.ppermute(own, "core", [(0, 1), (1, 0)])
    encode = call(
        encode_kernel, [VMEM], (8, 2 * STRIP, 2 * HALF), BF16, turned_scratch, moved=3 << 20
    )(first)
    shares = call(strip_kernel, [VMEM] * 3, (16, STRIP, STRIP), BF16, flops=1 << 29)(
        first, other, encode
    )
    gather, reduce = groups()
    line = ("core",) + FAC
    shares = lax.all_to_all(shares, ("xh", "y", "xl"), 0, 0)
    strip = call(
        sum_kernel,
        [VMEM],
        (4, 2 * STRIP, STRIP),
        BF16,
        [pltpu.VMEM((2 * STRIP, STRIP), BF16), pltpu.SemaphoreType.DMA((4,))],
        out=HBM,
    )(shares)
    strip, pack = lax.optimization_barrier((strip, pack))
    tables = (2 * STRIP, 4 * HALF)
    decode, spot = call(
        decode_kernel,
        [SMEM, VMEM],
        [(AHEAD, *tables), (8, STRIP)],
        [BF16, jnp.int32],
        turned_scratch,
        moved=3 << 20,
        out=[VMEM] * 2,
    )(column_place, pack)
    strips = lax.all_to_all(strip, line, 0, 0, axis_index_groups=gather)
    partial = call(
        subgrid_kernel,
        [VMEM] * 3,
        (8, STRIP, STRIP),
        BF16,
        [pltpu.VMEM((8 - AHEAD, *tables), BF16), *turned_scratch],
        flops=1 << 29,
    )(strips, decode, pack)
    received = lax.all_to_all(partial, line, 0, 0, axis_index_groups=reduce)
    subgrid = call(
        place_kernel,
        [VMEM, VMEM],
        (2, SUBGRID, STRIP),
        F32,
        [pltpu.VMEM((2, SUBGRID + STRIP, STRIP), F32), pltpu.SemaphoreType.DMA((2,))],
        out=HBM,
    )(spot, received)
    return subgrid.reshape(1, 1, 2, SUBGRID, STRIP)


def solution(mesh):
    split = Mesh(mesh.devices.reshape(SIZES), SPLIT)
    in_specs = (P(None, COL, FAC), P(COL), P(), P(), P(), P(), P())
    return jax.shard_map(
        on_device,
        mesh=split,
        in_specs=in_specs,
        out_specs=P(COL, FAC, None, None, None),
        check_vma=False,
    )
```

```python
import math

import jax
import jax.numpy as jnp
import numpy as np
from jax import lax
from jax.experimental import pallas as pl
from jax.experimental.pallas import tpu as pltpu
from jax.sharding import Mesh, PartitionSpec as P

FACET = 4096
STRIP = 128
SUBGRID = 512
HALF = 256
SPLIT = ("xh", "y", "core", "xl", "zh", "zl")
SIZES = (2, 4, 2, 2, 4, 4)
COL = SPLIT[:3]
FAC = SPLIT[3:]
RUN = (0, 1, 2, 3)
RUNS = ((2, 3, 0, 1), (2, 3, 0, 1))
TWIST = (0, 2, 2, 0)
MEMBERS = ((0, 0), (0, 1), (0, 2), (0, 3), (1, 0), (1, 1), (1, 2), (1, 3))
SHIFT = (2, 0)
F32 = jnp.float32
BF16 = jnp.bfloat16
VMEM = pl.BlockSpec(memory_space=pltpu.VMEM)
HBM = pl.BlockSpec(memory_space=pltpu.HBM)
SMEM = pl.BlockSpec(memory_space=pltpu.SMEM)
BASE = 48
ENCODE = slice(BASE, BASE + 8)
DECODE = slice(BASE + 8, BASE + 16)
OWN = slice(BASE + 16, BASE + 16 + HALF)
AHEAD = 6
NT = (((1,), (1,)), ((), ()))


def base_table():
    def rows(ks, scale):
        angle = (ks[:, None] * np.arange(HALF)[None, :] % FACET) * (2.0 * math.pi / FACET)
        return [np.cos(angle) * scale, -np.sin(angle) * scale]

    small, large = np.arange(16), 16 * np.arange(8)
    return np.concatenate(rows(small, 1.0) + rows(large, 1.0 / math.sqrt(FACET))).astype(np.float32)


def unit(phase):
    angle = phase.astype(F32) * (2.0 * math.pi / FACET)
    return jnp.cos(angle), -jnp.sin(angle)


def turned(pack_ref, turned_ref, block):
    k = lax.broadcasted_iota(jnp.int32, (16, HALF), 0)
    real, imag = unit((k * block & 15) * HALF)
    base_real, base_imag = pack_ref[0:16, :], pack_ref[16:32, :]
    real, imag = base_real * real - base_imag * imag, base_real * imag + base_imag * real
    for large in range(8):
        row_real = pack_ref[32 + large : 33 + large, :]
        row_imag = pack_ref[40 + large : 41 + large, :]
        rows = pl.ds(16 * large, 16)
        turned_ref[0, rows, :] = row_real * real - row_imag * imag
        turned_ref[1, rows, :] = row_real * imag + row_imag * real


def position():
    core, xl, zh, zl = (lax.axis_index(name) for name in ("core", "xl", "zh", "zl"))
    shift = jnp.where(core == 0, *SHIFT)
    place = (4 * zh + zl - shift) & 15
    return core, xl, place >> 2, place & 3, shift


def spread(starts):
    row = lax.broadcasted_iota(jnp.int32, (8, HALF), 0)
    first = jnp.zeros((8, HALF), jnp.int32)
    for n, start in enumerate(starts):
        first = jnp.where(row == n, start, first)
    return first.astype(F32)


def fill_tables(pack_ref, firsts, turn, blocks, outs, turned_ref):
    lane = lax.broadcasted_iota(jnp.int32, (8, HALF), 1)
    first = pack_ref[firsts].astype(jnp.int32)
    for c, block in enumerate(blocks):
        turned(pack_ref, turned_ref, block)
        real, imag = unit(first * (block * HALF + lane) & (FACET - 1))
        for k in range(0, STRIP, 16):
            rows = pl.ds(k, 16)
            base_real, base_imag = turned_ref[0, rows, :], turned_ref[1, rows, :]
            row = k // turn * 2 * turn + k % turn
            for n, out in outs.items():
                own_real, own_imag = real[n : n + 1], imag[n : n + 1]
                out[pl.ds(row, 16), HALF * c : HALF * (c + 1)] = (
                    own_real * base_real - own_imag * base_imag
                ).astype(BF16)
                out[pl.ds(row + turn, 16), HALF * c : HALF * (c + 1)] = (
                    own_real * base_imag + own_imag * base_real
                ).astype(BF16)


def prepare_kernel(
    facets_hbm,
    row_hbm,
    column_hbm,
    row_offset_hbm,
    offset_hbm,
    slot_hbm,
    base_hbm,
    out_hbm,
    first_hbm,
    pack_hbm,
    facets_ref,
    row_ref,
    column_ref,
    row_offset_ref,
    offset_ref,
    slot_ref,
    out_ref,
    pack_ref,
    sems,
    out_sems,
):
    core, xl, line, step, shift = position()
    pair = lax.axis_index("xh") * 4 + lax.axis_index("y")
    fac = (xl * 4 + lax.axis_index("zh")) * 4 + lax.axis_index("zl")
    copies = [
        pltpu.make_async_copy(source, target, sems.at[n])
        for n, (source, target) in enumerate(
            [
                (facets_hbm, facets_ref),
                (row_hbm, row_ref),
                (column_hbm, column_ref),
                (row_offset_hbm, row_offset_ref),
                (offset_hbm, offset_ref),
                (slot_hbm, slot_ref),
                (base_hbm, pack_ref.at[pl.ds(0, BASE)]),
            ]
        )
    ]
    for copy in copies:
        copy.start()
    for copy in copies[:3]:
        copy.wait()
    column = column_ref[pl.ds(fac, 1), :]
    for part in range(2):
        scaled = facets_ref[part].astype(F32) * column
        block = (scaled.T * row_ref[...]).astype(BF16)
        out_ref[STRIP * part : STRIP * (part + 1), :] = block
        pack_ref[BASE + 16 + STRIP * part : BASE + 16 + STRIP * (part + 1), :] = block.astype(F32)
    own_copy = pltpu.make_async_copy(out_ref, out_hbm, out_sems.at[0])
    own_copy.start()
    for copy in copies[3:6]:
        copy.wait()
    pack_ref[ENCODE] = spread([row_offset_ref[2 * n + core] for n in range(8)])
    slots = []
    twist = sum(jnp.where(line == n, TWIST[n], 0) for n in range(4))
    for first, second in zip(*RUNS):
        run = jnp.where(core == 0, first, second)
        away = jnp.where(core == 0, TWIST[first], TWIST[second])
        slots.append((4 * run + shift + ((step - twist + away) & 3)) & 15)
    slots = [slots[n] + 16 * side for side, n in MEMBERS]
    pack_ref[DECODE] = spread([offset_ref[slot_ref[2 * pair + core, slot] & 31] for slot in slots])
    copies[6].wait()
    first_copy = pltpu.make_async_copy(pack_ref, first_hbm, out_sems.at[1])
    first_copy.start()
    pack_copy = pltpu.make_async_copy(pack_ref.at[pl.ds(0, BASE + 16)], pack_hbm, out_sems.at[2])
    pack_copy.start()
    own_copy.wait()
    first_copy.wait()
    pack_copy.wait()


def encode_kernel(pack_ref, out_ref, turned_ref):
    core = lax.axis_index("core")
    pair = lax.axis_index("xh") * 4 + lax.axis_index("y")
    outs = {n: out_ref.at[n] for n in range(8)}
    blocks = [2 * pair + core, 2 * pair + 1 - core]
    fill_tables(pack_ref, ENCODE, STRIP // 2, blocks, outs, turned_ref)


def decode_tables(pack_ref, outs, turned_ref):
    _, _, line, _, shift = position()
    blocks = [8 * xl + ((2 * line + (shift >> 1) + half) & 7) for xl in range(2) for half in range(2)]
    fill_tables(pack_ref, DECODE, STRIP, blocks, outs, turned_ref)


def decode_kernel(place_ref, pack_ref, out_ref, spot_ref, turned_ref):
    spot_ref[...] = jnp.full((8, STRIP), place_ref[0], jnp.int32)
    decode_tables(pack_ref, {n: out_ref.at[n] for n in range(AHEAD)}, turned_ref)


def joined(real_rows, imag_rows):
    lane = lax.broadcasted_iota(jnp.int32, real_rows.shape, 1)
    turned = pltpu.roll(imag_rows, STRIP // 2, 1)
    return real_rows + jnp.where(lane < STRIP // 2, -turned, turned)


def strip_kernel(first_ref, other_ref, table_ref, out_ref):
    own = first_ref[OWN].astype(BF16)
    for n in range(8):
        product = lax.dot_general(
            own, table_ref[n, :, :HALF], NT, preferred_element_type=F32
        ) + lax.dot_general(
            other_ref[...], table_ref[n, :, HALF:], NT, preferred_element_type=F32
        )
        for half in range(2):
            part = product[:, STRIP * half : STRIP * (half + 1)]
            out_ref[2 * n + half] = joined(part[:STRIP], part[STRIP:]).astype(BF16)


def sum_kernel(parts_ref, out_hbm, total_ref, sems):
    for xl in range(2):
        total = parts_ref[xl].astype(F32)
        for n in range(1, 8):
            total += parts_ref[2 * n + xl].astype(F32)
        total_ref[STRIP * xl : STRIP * (xl + 1), :] = total.astype(BF16)
    copies = [pltpu.make_async_copy(total_ref, out_hbm.at[n], sems.at[n]) for n in range(4)]
    for copy in copies:
        copy.start()
    for copy in copies:
        copy.wait()


def subgrid_kernel(strip_ref, ahead_ref, pack_ref, out_ref, late_ref, turned_ref):
    decode_tables(pack_ref, {n: late_ref.at[n - AHEAD] for n in range(AHEAD, 8)}, turned_ref)
    strip = jnp.concatenate(
        [
            strip_ref[RUN.index(n), STRIP * xl : STRIP * (xl + 1), :]
            for xl in range(2)
            for n in range(4)
        ]
    )
    for n in range(8):
        table = ahead_ref[n] if n < AHEAD else late_ref[n - AHEAD]
        product = jnp.dot(table, strip, preferred_element_type=F32)
        out_ref[n] = joined(product[:STRIP], product[STRIP:]).astype(BF16)


def place_kernel(place_ref, parts_ref, out_hbm, scratch_ref, sems):
    place = jnp.max(place_ref[...]) & (SUBGRID - 1)
    scratch_ref[...] = jnp.zeros_like(scratch_ref)
    halves = []
    for xl in range(2):
        first, *others = [n for n in range(8) if MEMBERS[n][0] == xl]
        total = parts_ref[first].astype(F32)
        for n in others:
            total += parts_ref[n].astype(F32)
        halves.append(total)
    low = lax.broadcasted_iota(jnp.int32, (STRIP, STRIP), 1) < STRIP // 2
    copies = []
    for part in range(2):
        turned = pltpu.roll(halves[1 - part], STRIP // 2, 1)
        whole = jnp.where(low, turned, halves[1]) if part else jnp.where(low, halves[0], turned)
        scratch_ref[part, pl.ds(place, STRIP), :] = whole
        scratch_ref[part, :STRIP, :] += scratch_ref[part, SUBGRID:, :]
        copy = pltpu.make_async_copy(
            scratch_ref.at[part, pl.ds(0, SUBGRID)], out_hbm.at[part], sems.at[part]
        )
        copy.start()
        copies.append(copy)
    for copy in copies:
        copy.wait()


def call(kernel, specs, shape, dtype, scratch=(), flops=0, moved=1 << 20, out=VMEM):
    if isinstance(shape, list):
        result = [jax.ShapeDtypeStruct(*pair) for pair in zip(shape, dtype)]
    else:
        result = jax.ShapeDtypeStruct(shape, dtype)
    return pl.pallas_call(
        kernel,
        out_shape=result,
        in_specs=specs,
        out_specs=out,
        scratch_shapes=list(scratch),
        compiler_params=pltpu.CompilerParams(vmem_limit_bytes=24 * 1024 * 1024),
        cost_estimate=pl.CostEstimate(flops=flops, bytes_accessed=moved, transcendentals=0),
    )


def prepare(*operands):
    return pl.pallas_call(
        prepare_kernel,
        out_shape=(
            jax.ShapeDtypeStruct((2 * STRIP, HALF), BF16),
            jax.ShapeDtypeStruct((BASE + 16 + HALF, HALF), F32),
            jax.ShapeDtypeStruct((BASE + 16, HALF), F32),
        ),
        in_specs=[HBM] * 7,
        out_specs=(HBM, HBM, HBM),
        scratch_shapes=[
            pltpu.VMEM((2, HALF, STRIP), BF16),
            pltpu.VMEM((1, HALF), F32),
            pltpu.VMEM((32, STRIP), F32),
            pltpu.SMEM((16,), jnp.int32),
            pltpu.SMEM((32,), jnp.int32),
            pltpu.SMEM((16, 32), jnp.int32),
            pltpu.VMEM((2 * STRIP, HALF), BF16),
            pltpu.VMEM((BASE + 16 + HALF, HALF), F32),
            pltpu.SemaphoreType.DMA((7,)),
            pltpu.SemaphoreType.DMA((3,)),
        ],
        compiler_params=pltpu.CompilerParams(vmem_limit_bytes=60 * 1024 * 1024),
        cost_estimate=pl.CostEstimate(flops=0, bytes_accessed=1 << 20, transcendentals=0),
    )(*operands)


def groups():
    gather = [
        [32 * core + 16 * xl + (4 * n + SHIFT[core] + j) % 16 for j in RUN]
        for core in range(2)
        for xl in range(2)
        for n in range(4)
    ]
    reduce = [
        [
            32 * core + 16 * xl + (4 * n + SHIFT[core] + (s + TWIST[n]) % 4) % 16
            for xl, n in ((xl, RUNS[core][n]) for xl, n in MEMBERS)
        ]
        for core in range(2)
        for s in range(4)
    ]
    return gather, reduce


def on_device(
    facets, row_taper, column_taper, column_place, row_offset, column_offset, slot_subgrid
):
    turned_scratch = [pltpu.VMEM((2, STRIP, HALF), F32)]
    own, first, pack = prepare(
        facets,
        row_taper.reshape(1, HALF),
        column_taper.reshape(32, STRIP),
        row_offset,
        column_offset,
        slot_subgrid,
        jnp.asarray(base_table()),
    )
    other = lax.ppermute(own, "core", [(0, 1), (1, 0)])
    encode = call(
        encode_kernel, [VMEM], (8, 2 * STRIP, 2 * HALF), BF16, turned_scratch, moved=3 << 20
    )(first)
    shares = call(strip_kernel, [VMEM] * 3, (16, STRIP, STRIP), BF16, flops=1 << 29)(
        first, other, encode
    )
    gather, reduce = groups()
    line = ("core",) + FAC
    shares = lax.all_to_all(shares, ("xh", "y", "xl"), 0, 0)
    strip = call(
        sum_kernel,
        [VMEM],
        (4, 2 * STRIP, STRIP),
        BF16,
        [pltpu.VMEM((2 * STRIP, STRIP), BF16), pltpu.SemaphoreType.DMA((4,))],
        out=HBM,
    )(shares)
    strip, pack = lax.optimization_barrier((strip, pack))
    tables = (2 * STRIP, 4 * HALF)
    decode, spot = call(
        decode_kernel,
        [SMEM, VMEM],
        [(AHEAD, *tables), (8, STRIP)],
        [BF16, jnp.int32],
        turned_scratch,
        moved=3 << 20,
        out=[VMEM] * 2,
    )(column_place, pack)
    strips = lax.all_to_all(strip, line, 0, 0, axis_index_groups=gather)
    partial = call(
        subgrid_kernel,
        [VMEM] * 3,
        (8, STRIP, STRIP),
        BF16,
        [pltpu.VMEM((8 - AHEAD, *tables), BF16), *turned_scratch],
        flops=1 << 29,
    )(strips, decode, pack)
    received = lax.all_to_all(partial, line, 0, 0, axis_index_groups=reduce)
    subgrid = call(
        place_kernel,
        [VMEM, VMEM],
        (2, SUBGRID, STRIP),
        F32,
        [pltpu.VMEM((2, SUBGRID + STRIP, STRIP), F32), pltpu.SemaphoreType.DMA((2,))],
        out=HBM,
    )(spot, received)
    return subgrid.reshape(1, 1, 2, SUBGRID, STRIP)


def solution(mesh):
    split = Mesh(mesh.devices.reshape(SIZES), SPLIT)
    in_specs = (P(None, COL, FAC), P(COL), P(), P(), P(), P(), P())
    return jax.shard_map(
        on_device,
        mesh=split,
        in_specs=in_specs,
        out_specs=P(COL, FAC, None, None, None),
        check_vma=False,
    )
```

```python
import math

import jax
import jax.numpy as jnp
import numpy as np
from jax import lax
from jax.experimental import pallas as pl
from jax.experimental.pallas import tpu as pltpu
from jax.sharding import Mesh, PartitionSpec as P

FACET = 4096
STRIP = 128
SUBGRID = 512
HALF = 256
SPLIT = ("xh", "y", "core", "xl", "zh", "zl")
SIZES = (2, 4, 2, 2, 4, 4)
COL = SPLIT[:3]
FAC = SPLIT[3:]
PLANE = tuple(range(15, -1, -1))
RUN = (0, 1, 2, 3)
RUNS = ((2, 3, 1, 0), (2, 3, 1, 0))
TWIST = (0, 2, 2, 0)
MEMBERS = ((0, 0), (0, 1), (0, 2), (0, 3), (1, 0), (1, 1), (1, 2), (1, 3))
SHIFT = (2, 0)
F32 = jnp.float32
BF16 = jnp.bfloat16
VMEM = pl.BlockSpec(memory_space=pltpu.VMEM)
HBM = pl.BlockSpec(memory_space=pltpu.HBM)
SMEM = pl.BlockSpec(memory_space=pltpu.SMEM)
BASE = 48
ENCODE = slice(BASE, BASE + 8)
DECODE = slice(BASE + 8, BASE + 16)
OWN = slice(BASE + 16, BASE + 16 + HALF)
AHEAD = 6
NT = (((1,), (1,)), ((), ()))


def base_table():
    def rows(ks, scale):
        angle = (ks[:, None] * np.arange(HALF)[None, :] % FACET) * (2.0 * math.pi / FACET)
        return [np.cos(angle) * scale, -np.sin(angle) * scale]

    small, large = np.arange(16), 16 * np.arange(8)
    return np.concatenate(rows(small, 1.0) + rows(large, 1.0 / math.sqrt(FACET))).astype(np.float32)


def unit(phase):
    angle = phase.astype(F32) * (2.0 * math.pi / FACET)
    return jnp.cos(angle), -jnp.sin(angle)


def turned(pack_ref, turned_ref, block):
    k = lax.broadcasted_iota(jnp.int32, (16, HALF), 0)
    real, imag = unit((k * block & 15) * HALF)
    base_real, base_imag = pack_ref[0:16, :], pack_ref[16:32, :]
    real, imag = base_real * real - base_imag * imag, base_real * imag + base_imag * real
    for large in range(8):
        row_real = pack_ref[32 + large : 33 + large, :]
        row_imag = pack_ref[40 + large : 41 + large, :]
        rows = pl.ds(16 * large, 16)
        turned_ref[0, rows, :] = row_real * real - row_imag * imag
        turned_ref[1, rows, :] = row_real * imag + row_imag * real


def position():
    core, xl, zh, zl = (lax.axis_index(name) for name in ("core", "xl", "zh", "zl"))
    shift = jnp.where(core == 0, *SHIFT)
    place = (4 * zh + zl - shift) & 15
    return core, xl, place >> 2, place & 3, shift


def spread(starts):
    row = lax.broadcasted_iota(jnp.int32, (8, HALF), 0)
    first = jnp.zeros((8, HALF), jnp.int32)
    for n, start in enumerate(starts):
        first = jnp.where(row == n, start, first)
    return first.astype(F32)


def fill_tables(pack_ref, firsts, turn, blocks, outs, turned_ref):
    lane = lax.broadcasted_iota(jnp.int32, (8, HALF), 1)
    first = pack_ref[firsts].astype(jnp.int32)
    for c, block in enumerate(blocks):
        turned(pack_ref, turned_ref, block)
        real, imag = unit(first * (block * HALF + lane) & (FACET - 1))
        for k in range(0, STRIP, 16):
            rows = pl.ds(k, 16)
            base_real, base_imag = turned_ref[0, rows, :], turned_ref[1, rows, :]
            row = k // turn * 2 * turn + k % turn
            for n, out in outs.items():
                own_real, own_imag = real[n : n + 1], imag[n : n + 1]
                out[pl.ds(row, 16), HALF * c : HALF * (c + 1)] = (
                    own_real * base_real - own_imag * base_imag
                ).astype(BF16)
                out[pl.ds(row + turn, 16), HALF * c : HALF * (c + 1)] = (
                    own_real * base_imag + own_imag * base_real
                ).astype(BF16)


def prepare_kernel(
    facets_hbm,
    row_hbm,
    column_hbm,
    row_offset_hbm,
    offset_hbm,
    slot_hbm,
    base_hbm,
    out_hbm,
    first_hbm,
    pack_hbm,
    facets_ref,
    row_ref,
    column_ref,
    row_offset_ref,
    offset_ref,
    slot_ref,
    out_ref,
    pack_ref,
    sems,
    out_sems,
):
    core, xl, line, step, shift = position()
    pair = lax.axis_index("xh") * 4 + lax.axis_index("y")
    fac = (xl * 4 + lax.axis_index("zh")) * 4 + lax.axis_index("zl")
    copies = [
        pltpu.make_async_copy(source, target, sems.at[n])
        for n, (source, target) in enumerate(
            [
                (facets_hbm, facets_ref),
                (row_hbm, row_ref),
                (column_hbm, column_ref),
                (row_offset_hbm, row_offset_ref),
                (offset_hbm, offset_ref),
                (slot_hbm, slot_ref),
                (base_hbm, pack_ref.at[pl.ds(0, BASE)]),
            ]
        )
    ]
    for copy in copies:
        copy.start()
    for copy in copies[:3]:
        copy.wait()
    column = column_ref[pl.ds(fac, 1), :]
    for part in range(2):
        scaled = facets_ref[part].astype(F32) * column
        block = (scaled.T * row_ref[...]).astype(BF16)
        out_ref[STRIP * part : STRIP * (part + 1), :] = block
        pack_ref[BASE + 16 + STRIP * part : BASE + 16 + STRIP * (part + 1), :] = block.astype(F32)
    own_copy = pltpu.make_async_copy(out_ref, out_hbm, out_sems.at[0])
    own_copy.start()
    for copy in copies[3:6]:
        copy.wait()
    pack_ref[ENCODE] = spread([row_offset_ref[2 * n + core] for n in range(8)])
    slots = []
    twist = sum(jnp.where(line == n, TWIST[n], 0) for n in range(4))
    for first, second in zip(*RUNS):
        run = jnp.where(core == 0, first, second)
        away = jnp.where(core == 0, TWIST[first], TWIST[second])
        slots.append((4 * run + shift + ((step - twist + away) & 3)) & 15)
    slots = [slots[n] + 16 * side for side, n in MEMBERS]
    pack_ref[DECODE] = spread([offset_ref[slot_ref[2 * pair + core, slot] & 31] for slot in slots])
    copies[6].wait()
    first_copy = pltpu.make_async_copy(pack_ref, first_hbm, out_sems.at[1])
    first_copy.start()
    pack_copy = pltpu.make_async_copy(pack_ref.at[pl.ds(0, BASE + 16)], pack_hbm, out_sems.at[2])
    pack_copy.start()
    own_copy.wait()
    first_copy.wait()
    pack_copy.wait()


def encode_kernel(pack_ref, out_ref, turned_ref):
    core = lax.axis_index("core")
    pair = lax.axis_index("xh") * 4 + lax.axis_index("y")
    outs = {n: out_ref.at[n] for n in range(8)}
    blocks = [2 * pair + core, 2 * pair + 1 - core]
    fill_tables(pack_ref, ENCODE, STRIP // 2, blocks, outs, turned_ref)


def decode_tables(pack_ref, outs, turned_ref):
    _, _, line, _, shift = position()
    blocks = [8 * xl + ((2 * line + (shift >> 1) + half) & 7) for xl in range(2) for half in range(2)]
    fill_tables(pack_ref, DECODE, STRIP, blocks, outs, turned_ref)


def decode_kernel(place_ref, pack_ref, out_ref, spot_ref, turned_ref):
    spot_ref[...] = jnp.full((8, STRIP), place_ref[0], jnp.int32)
    decode_tables(pack_ref, {n: out_ref.at[n] for n in range(AHEAD)}, turned_ref)


def joined(real_rows, imag_rows):
    lane = lax.broadcasted_iota(jnp.int32, real_rows.shape, 1)
    turned = pltpu.roll(imag_rows, STRIP // 2, 1)
    return real_rows + jnp.where(lane < STRIP // 2, -turned, turned)


def strip_kernel(first_ref, other_ref, table_ref, out_ref):
    own = first_ref[OWN].astype(BF16)
    for n in range(8):
        product = lax.dot_general(
            own, table_ref[n, :, :HALF], NT, preferred_element_type=F32
        ) + lax.dot_general(
            other_ref[...], table_ref[n, :, HALF:], NT, preferred_element_type=F32
        )
        for half in range(2):
            part = product[:, STRIP * half : STRIP * (half + 1)]
            out_ref[PLANE.index(2 * n + half)] = joined(part[:STRIP], part[STRIP:]).astype(BF16)


def sum_kernel(parts_ref, out_hbm, total_ref, sems):
    for xl in range(2):
        first, *others = [PLANE.index(2 * n + xl) for n in range(8)]
        total = parts_ref[first].astype(F32)
        for n in others:
            total += parts_ref[n].astype(F32)
        total_ref[STRIP * xl : STRIP * (xl + 1), :] = total.astype(BF16)
    copies = [pltpu.make_async_copy(total_ref, out_hbm.at[n], sems.at[n]) for n in range(4)]
    for copy in copies:
        copy.start()
    for copy in copies:
        copy.wait()


def subgrid_kernel(strip_ref, ahead_ref, pack_ref, out_ref, late_ref, turned_ref):
    decode_tables(pack_ref, {n: late_ref.at[n - AHEAD] for n in range(AHEAD, 8)}, turned_ref)
    strip = jnp.concatenate(
        [
            strip_ref[RUN.index(n), STRIP * xl : STRIP * (xl + 1), :]
            for xl in range(2)
            for n in range(4)
        ]
    )
    for n in range(8):
        table = ahead_ref[n] if n < AHEAD else late_ref[n - AHEAD]
        product = jnp.dot(table, strip, preferred_element_type=F32)
        out_ref[n] = joined(product[:STRIP], product[STRIP:]).astype(BF16)


def place_kernel(place_ref, parts_ref, out_hbm, scratch_ref, sems):
    place = jnp.max(place_ref[...]) & (SUBGRID - 1)
    scratch_ref[...] = jnp.zeros_like(scratch_ref)
    halves = []
    for xl in range(2):
        first, *others = [n for n in range(8) if MEMBERS[n][0] == xl]
        total = parts_ref[first].astype(F32)
        for n in others:
            total += parts_ref[n].astype(F32)
        halves.append(total)
    low = lax.broadcasted_iota(jnp.int32, (STRIP, STRIP), 1) < STRIP // 2
    copies = []
    for part in range(2):
        turned = pltpu.roll(halves[1 - part], STRIP // 2, 1)
        whole = jnp.where(low, turned, halves[1]) if part else jnp.where(low, halves[0], turned)
        scratch_ref[part, pl.ds(place, STRIP), :] = whole
        scratch_ref[part, :STRIP, :] += scratch_ref[part, SUBGRID:, :]
        copy = pltpu.make_async_copy(
            scratch_ref.at[part, pl.ds(0, SUBGRID)], out_hbm.at[part], sems.at[part]
        )
        copy.start()
        copies.append(copy)
    for copy in copies:
        copy.wait()


def call(kernel, specs, shape, dtype, scratch=(), flops=0, moved=1 << 20, out=VMEM):
    if isinstance(shape, list):
        result = [jax.ShapeDtypeStruct(*pair) for pair in zip(shape, dtype)]
    else:
        result = jax.ShapeDtypeStruct(shape, dtype)
    return pl.pallas_call(
        kernel,
        out_shape=result,
        in_specs=specs,
        out_specs=out,
        scratch_shapes=list(scratch),
        compiler_params=pltpu.CompilerParams(vmem_limit_bytes=24 * 1024 * 1024),
        cost_estimate=pl.CostEstimate(flops=flops, bytes_accessed=moved, transcendentals=0),
    )


def prepare(*operands):
    return pl.pallas_call(
        prepare_kernel,
        out_shape=(
            jax.ShapeDtypeStruct((2 * STRIP, HALF), BF16),
            jax.ShapeDtypeStruct((BASE + 16 + HALF, HALF), F32),
            jax.ShapeDtypeStruct((BASE + 16, HALF), F32),
        ),
        in_specs=[HBM] * 7,
        out_specs=(HBM, HBM, HBM),
        scratch_shapes=[
            pltpu.VMEM((2, HALF, STRIP), BF16),
            pltpu.VMEM((1, HALF), F32),
            pltpu.VMEM((32, STRIP), F32),
            pltpu.SMEM((16,), jnp.int32),
            pltpu.SMEM((32,), jnp.int32),
            pltpu.SMEM((16, 32), jnp.int32),
            pltpu.VMEM((2 * STRIP, HALF), BF16),
            pltpu.VMEM((BASE + 16 + HALF, HALF), F32),
            pltpu.SemaphoreType.DMA((7,)),
            pltpu.SemaphoreType.DMA((3,)),
        ],
        compiler_params=pltpu.CompilerParams(vmem_limit_bytes=60 * 1024 * 1024),
        cost_estimate=pl.CostEstimate(flops=0, bytes_accessed=1 << 20, transcendentals=0),
    )(*operands)


def groups():
    gather = [
        [32 * core + 16 * xl + (4 * n + SHIFT[core] + j) % 16 for j in RUN]
        for core in range(2)
        for xl in range(2)
        for n in range(4)
    ]
    reduce = [
        [
            32 * core + 16 * xl + (4 * n + SHIFT[core] + (s + TWIST[n]) % 4) % 16
            for xl, n in ((xl, RUNS[core][n]) for xl, n in MEMBERS)
        ]
        for core in range(2)
        for s in range(4)
    ]
    return gather, reduce


def on_device(
    facets, row_taper, column_taper, column_place, row_offset, column_offset, slot_subgrid
):
    turned_scratch = [pltpu.VMEM((2, STRIP, HALF), F32)]
    own, first, pack = prepare(
        facets,
        row_taper.reshape(1, HALF),
        column_taper.reshape(32, STRIP),
        row_offset,
        column_offset,
        slot_subgrid,
        jnp.asarray(base_table()),
    )
    other = lax.ppermute(own, "core", [(0, 1), (1, 0)])
    encode = call(
        encode_kernel, [VMEM], (8, 2 * STRIP, 2 * HALF), BF16, turned_scratch, moved=3 << 20
    )(first)
    shares = call(strip_kernel, [VMEM] * 3, (16, STRIP, STRIP), BF16, flops=1 << 29)(
        first, other, encode
    )
    gather, reduce = groups()
    line = ("core",) + FAC
    shares = lax.all_to_all(shares, ("xh", "y", "xl"), 0, 0, axis_index_groups=[list(PLANE)])
    strip = call(
        sum_kernel,
        [VMEM],
        (4, 2 * STRIP, STRIP),
        BF16,
        [pltpu.VMEM((2 * STRIP, STRIP), BF16), pltpu.SemaphoreType.DMA((4,))],
        out=HBM,
    )(shares)
    strip, pack = lax.optimization_barrier((strip, pack))
    tables = (2 * STRIP, 4 * HALF)
    decode, spot = call(
        decode_kernel,
        [SMEM, VMEM],
        [(AHEAD, *tables), (8, STRIP)],
        [BF16, jnp.int32],
        turned_scratch,
        moved=3 << 20,
        out=[VMEM] * 2,
    )(column_place, pack)
    strips = lax.all_to_all(strip, line, 0, 0, axis_index_groups=gather)
    partial = call(
        subgrid_kernel,
        [VMEM] * 3,
        (8, STRIP, STRIP),
        BF16,
        [pltpu.VMEM((8 - AHEAD, *tables), BF16), *turned_scratch],
        flops=1 << 29,
    )(strips, decode, pack)
    received = lax.all_to_all(partial, line, 0, 0, axis_index_groups=reduce)
    subgrid = call(
        place_kernel,
        [VMEM, VMEM],
        (2, SUBGRID, STRIP),
        F32,
        [pltpu.VMEM((2, SUBGRID + STRIP, STRIP), F32), pltpu.SemaphoreType.DMA((2,))],
        out=HBM,
    )(spot, received)
    return subgrid.reshape(1, 1, 2, SUBGRID, STRIP)


def solution(mesh):
    split = Mesh(mesh.devices.reshape(SIZES), SPLIT)
    in_specs = (P(None, COL, FAC), P(COL), P(), P(), P(), P(), P())
    return jax.shard_map(
        on_device,
        mesh=split,
        in_specs=in_specs,
        out_specs=P(COL, FAC, None, None, None),
        check_vma=False,
    )
```

```python
import math

import jax
import jax.numpy as jnp
import numpy as np
from jax import lax
from jax.experimental import pallas as pl
from jax.experimental.pallas import tpu as pltpu
from jax.sharding import Mesh, PartitionSpec as P

FACET = 4096
STRIP = 128
SUBGRID = 512
HALF = 256
SPLIT = ("xh", "y", "core", "xl", "zh", "zl")
SIZES = (2, 4, 2, 2, 4, 4)
COL = SPLIT[:3]
FAC = SPLIT[3:]
PLANE = (13, 12, 15, 14, 9, 8, 11, 10, 5, 4, 7, 6, 1, 0, 3, 2)
RUN = (0, 1, 2, 3)
RUNS = ((2, 3, 1, 0), (2, 3, 1, 0))
TWIST = (0, 2, 2, 0)
MEMBERS = ((0, 0), (0, 1), (0, 2), (0, 3), (1, 0), (1, 1), (1, 2), (1, 3))
SHIFT = (2, 0)
F32 = jnp.float32
BF16 = jnp.bfloat16
VMEM = pl.BlockSpec(memory_space=pltpu.VMEM)
HBM = pl.BlockSpec(memory_space=pltpu.HBM)
SMEM = pl.BlockSpec(memory_space=pltpu.SMEM)
BASE = 48
ENCODE = slice(BASE, BASE + 8)
DECODE = slice(BASE + 8, BASE + 16)
OWN = slice(BASE + 16, BASE + 16 + HALF)
AHEAD = 6
NT = (((1,), (1,)), ((), ()))


def base_table():
    def rows(ks, scale):
        angle = (ks[:, None] * np.arange(HALF)[None, :] % FACET) * (2.0 * math.pi / FACET)
        return [np.cos(angle) * scale, -np.sin(angle) * scale]

    small, large = np.arange(16), 16 * np.arange(8)
    return np.concatenate(rows(small, 1.0) + rows(large, 1.0 / math.sqrt(FACET))).astype(np.float32)


def unit(phase):
    angle = phase.astype(F32) * (2.0 * math.pi / FACET)
    return jnp.cos(angle), -jnp.sin(angle)


def turned(pack_ref, turned_ref, block):
    k = lax.broadcasted_iota(jnp.int32, (16, HALF), 0)
    real, imag = unit((k * block & 15) * HALF)
    base_real, base_imag = pack_ref[0:16, :], pack_ref[16:32, :]
    real, imag = base_real * real - base_imag * imag, base_real * imag + base_imag * real
    for large in range(8):
        row_real = pack_ref[32 + large : 33 + large, :]
        row_imag = pack_ref[40 + large : 41 + large, :]
        rows = pl.ds(16 * large, 16)
        turned_ref[0, rows, :] = row_real * real - row_imag * imag
        turned_ref[1, rows, :] = row_real * imag + row_imag * real


def position():
    core, xl, zh, zl = (lax.axis_index(name) for name in ("core", "xl", "zh", "zl"))
    shift = jnp.where(core == 0, *SHIFT)
    place = (4 * zh + zl - shift) & 15
    return core, xl, place >> 2, place & 3, shift


def spread(starts):
    row = lax.broadcasted_iota(jnp.int32, (8, HALF), 0)
    first = jnp.zeros((8, HALF), jnp.int32)
    for n, start in enumerate(starts):
        first = jnp.where(row == n, start, first)
    return first.astype(F32)


def fill_tables(pack_ref, firsts, turn, blocks, outs, turned_ref):
    lane = lax.broadcasted_iota(jnp.int32, (8, HALF), 1)
    first = pack_ref[firsts].astype(jnp.int32)
    for c, block in enumerate(blocks):
        turned(pack_ref, turned_ref, block)
        real, imag = unit(first * (block * HALF + lane) & (FACET - 1))
        for k in range(0, STRIP, 16):
            rows = pl.ds(k, 16)
            base_real, base_imag = turned_ref[0, rows, :], turned_ref[1, rows, :]
            row = k // turn * 2 * turn + k % turn
            for n, out in outs.items():
                own_real, own_imag = real[n : n + 1], imag[n : n + 1]
                out[pl.ds(row, 16), HALF * c : HALF * (c + 1)] = (
                    own_real * base_real - own_imag * base_imag
                ).astype(BF16)
                out[pl.ds(row + turn, 16), HALF * c : HALF * (c + 1)] = (
                    own_real * base_imag + own_imag * base_real
                ).astype(BF16)


def prepare_kernel(
    facets_hbm,
    row_hbm,
    column_hbm,
    row_offset_hbm,
    offset_hbm,
    slot_hbm,
    base_hbm,
    out_hbm,
    first_hbm,
    pack_hbm,
    facets_ref,
    row_ref,
    column_ref,
    row_offset_ref,
    offset_ref,
    slot_ref,
    out_ref,
    pack_ref,
    sems,
    out_sems,
):
    core, xl, line, step, shift = position()
    pair = lax.axis_index("xh") * 4 + lax.axis_index("y")
    fac = (xl * 4 + lax.axis_index("zh")) * 4 + lax.axis_index("zl")
    copies = [
        pltpu.make_async_copy(source, target, sems.at[n])
        for n, (source, target) in enumerate(
            [
                (facets_hbm, facets_ref),
                (row_hbm, row_ref),
                (column_hbm, column_ref),
                (row_offset_hbm, row_offset_ref),
                (offset_hbm, offset_ref),
                (slot_hbm, slot_ref),
                (base_hbm, pack_ref.at[pl.ds(0, BASE)]),
            ]
        )
    ]
    for copy in copies:
        copy.start()
    for copy in copies[:3]:
        copy.wait()
    column = column_ref[pl.ds(fac, 1), :]
    for part in range(2):
        scaled = facets_ref[part].astype(F32) * column
        block = (scaled.T * row_ref[...]).astype(BF16)
        out_ref[STRIP * part : STRIP * (part + 1), :] = block
        pack_ref[BASE + 16 + STRIP * part : BASE + 16 + STRIP * (part + 1), :] = block.astype(F32)
    own_copy = pltpu.make_async_copy(out_ref, out_hbm, out_sems.at[0])
    own_copy.start()
    for copy in copies[3:6]:
        copy.wait()
    pack_ref[ENCODE] = spread([row_offset_ref[2 * n + core] for n in range(8)])
    slots = []
    twist = sum(jnp.where(line == n, TWIST[n], 0) for n in range(4))
    for first, second in zip(*RUNS):
        run = jnp.where(core == 0, first, second)
        away = jnp.where(core == 0, TWIST[first], TWIST[second])
        slots.append((4 * run + shift + ((step - twist + away) & 3)) & 15)
    slots = [slots[n] + 16 * side for side, n in MEMBERS]
    pack_ref[DECODE] = spread([offset_ref[slot_ref[2 * pair + core, slot] & 31] for slot in slots])
    copies[6].wait()
    first_copy = pltpu.make_async_copy(pack_ref, first_hbm, out_sems.at[1])
    first_copy.start()
    pack_copy = pltpu.make_async_copy(pack_ref.at[pl.ds(0, BASE + 16)], pack_hbm, out_sems.at[2])
    pack_copy.start()
    own_copy.wait()
    first_copy.wait()
    pack_copy.wait()


def encode_kernel(pack_ref, out_ref, turned_ref):
    core = lax.axis_index("core")
    pair = lax.axis_index("xh") * 4 + lax.axis_index("y")
    outs = {n: out_ref.at[n] for n in range(8)}
    blocks = [2 * pair + core, 2 * pair + 1 - core]
    fill_tables(pack_ref, ENCODE, STRIP // 2, blocks, outs, turned_ref)


def decode_tables(pack_ref, outs, turned_ref):
    _, _, line, _, shift = position()
    blocks = [8 * xl + ((2 * line + (shift >> 1) + half) & 7) for xl in range(2) for half in range(2)]
    fill_tables(pack_ref, DECODE, STRIP, blocks, outs, turned_ref)


def decode_kernel(place_ref, pack_ref, out_ref, spot_ref, turned_ref):
    spot_ref[...] = jnp.full((8, STRIP), place_ref[0], jnp.int32)
    decode_tables(pack_ref, {n: out_ref.at[n] for n in range(AHEAD)}, turned_ref)


def joined(real_rows, imag_rows):
    lane = lax.broadcasted_iota(jnp.int32, real_rows.shape, 1)
    turned = pltpu.roll(imag_rows, STRIP // 2, 1)
    return real_rows + jnp.where(lane < STRIP // 2, -turned, turned)


def strip_kernel(first_ref, other_ref, table_ref, out_ref):
    own = first_ref[OWN].astype(BF16)
    for n in range(8):
        product = lax.dot_general(
            own, table_ref[n, :, :HALF], NT, preferred_element_type=F32
        ) + lax.dot_general(
            other_ref[...], table_ref[n, :, HALF:], NT, preferred_element_type=F32
        )
        for half in range(2):
            part = product[:, STRIP * half : STRIP * (half + 1)]
            out_ref[PLANE.index(2 * n + half)] = joined(part[:STRIP], part[STRIP:]).astype(BF16)


def sum_kernel(parts_ref, out_hbm, total_ref, sems):
    for xl in range(2):
        first, *others = [PLANE.index(2 * n + xl) for n in range(8)]
        total = parts_ref[first].astype(F32)
        for n in others:
            total += parts_ref[n].astype(F32)
        total_ref[STRIP * xl : STRIP * (xl + 1), :] = total.astype(BF16)
    copies = [pltpu.make_async_copy(total_ref, out_hbm.at[n], sems.at[n]) for n in range(4)]
    for copy in copies:
        copy.start()
    for copy in copies:
        copy.wait()


def subgrid_kernel(strip_ref, ahead_ref, pack_ref, out_ref, late_ref, turned_ref):
    decode_tables(pack_ref, {n: late_ref.at[n - AHEAD] for n in range(AHEAD, 8)}, turned_ref)
    strip = jnp.concatenate(
        [
            strip_ref[RUN.index(n), STRIP * xl : STRIP * (xl + 1), :]
            for xl in range(2)
            for n in range(4)
        ]
    )
    for n in range(8):
        table = ahead_ref[n] if n < AHEAD else late_ref[n - AHEAD]
        product = jnp.dot(table, strip, preferred_element_type=F32)
        out_ref[n] = joined(product[:STRIP], product[STRIP:]).astype(BF16)


def place_kernel(place_ref, parts_ref, out_hbm, scratch_ref, sems):
    place = jnp.max(place_ref[...]) & (SUBGRID - 1)
    scratch_ref[...] = jnp.zeros_like(scratch_ref)
    halves = []
    for xl in range(2):
        first, *others = [n for n in range(8) if MEMBERS[n][0] == xl]
        total = parts_ref[first].astype(F32)
        for n in others:
            total += parts_ref[n].astype(F32)
        halves.append(total)
    low = lax.broadcasted_iota(jnp.int32, (STRIP, STRIP), 1) < STRIP // 2
    copies = []
    for part in range(2):
        turned = pltpu.roll(halves[1 - part], STRIP // 2, 1)
        whole = jnp.where(low, turned, halves[1]) if part else jnp.where(low, halves[0], turned)
        scratch_ref[part, pl.ds(place, STRIP), :] = whole
        scratch_ref[part, :STRIP, :] += scratch_ref[part, SUBGRID:, :]
        copy = pltpu.make_async_copy(
            scratch_ref.at[part, pl.ds(0, SUBGRID)], out_hbm.at[part], sems.at[part]
        )
        copy.start()
        copies.append(copy)
    for copy in copies:
        copy.wait()


def call(kernel, specs, shape, dtype, scratch=(), flops=0, moved=1 << 20, out=VMEM):
    if isinstance(shape, list):
        result = [jax.ShapeDtypeStruct(*pair) for pair in zip(shape, dtype)]
    else:
        result = jax.ShapeDtypeStruct(shape, dtype)
    return pl.pallas_call(
        kernel,
        out_shape=result,
        in_specs=specs,
        out_specs=out,
        scratch_shapes=list(scratch),
        compiler_params=pltpu.CompilerParams(vmem_limit_bytes=24 * 1024 * 1024),
        cost_estimate=pl.CostEstimate(flops=flops, bytes_accessed=moved, transcendentals=0),
    )


def prepare(*operands):
    return pl.pallas_call(
        prepare_kernel,
        out_shape=(
            jax.ShapeDtypeStruct((2 * STRIP, HALF), BF16),
            jax.ShapeDtypeStruct((BASE + 16 + HALF, HALF), F32),
            jax.ShapeDtypeStruct((BASE + 16, HALF), F32),
        ),
        in_specs=[HBM] * 7,
        out_specs=(HBM, HBM, HBM),
        scratch_shapes=[
            pltpu.VMEM((2, HALF, STRIP), BF16),
            pltpu.VMEM((1, HALF), F32),
            pltpu.VMEM((32, STRIP), F32),
            pltpu.SMEM((16,), jnp.int32),
            pltpu.SMEM((32,), jnp.int32),
            pltpu.SMEM((16, 32), jnp.int32),
            pltpu.VMEM((2 * STRIP, HALF), BF16),
            pltpu.VMEM((BASE + 16 + HALF, HALF), F32),
            pltpu.SemaphoreType.DMA((7,)),
            pltpu.SemaphoreType.DMA((3,)),
        ],
        compiler_params=pltpu.CompilerParams(vmem_limit_bytes=60 * 1024 * 1024),
        cost_estimate=pl.CostEstimate(flops=0, bytes_accessed=1 << 20, transcendentals=0),
    )(*operands)


def groups():
    gather = [
        [32 * core + 16 * xl + (4 * n + SHIFT[core] + j) % 16 for j in RUN]
        for core in range(2)
        for xl in range(2)
        for n in range(4)
    ]
    reduce = [
        [
            32 * core + 16 * xl + (4 * n + SHIFT[core] + (s + TWIST[n]) % 4) % 16
            for xl, n in ((xl, RUNS[core][n]) for xl, n in MEMBERS)
        ]
        for core in range(2)
        for s in range(4)
    ]
    return gather, reduce


def on_device(
    facets, row_taper, column_taper, column_place, row_offset, column_offset, slot_subgrid
):
    turned_scratch = [pltpu.VMEM((2, STRIP, HALF), F32)]
    own, first, pack = prepare(
        facets,
        row_taper.reshape(1, HALF),
        column_taper.reshape(32, STRIP),
        row_offset,
        column_offset,
        slot_subgrid,
        jnp.asarray(base_table()),
    )
    other = lax.ppermute(own, "core", [(0, 1), (1, 0)])
    encode = call(
        encode_kernel, [VMEM], (8, 2 * STRIP, 2 * HALF), BF16, turned_scratch, moved=3 << 20
    )(first)
    shares = call(strip_kernel, [VMEM] * 3, (16, STRIP, STRIP), BF16, flops=1 << 29)(
        first, other, encode
    )
    gather, reduce = groups()
    line = ("core",) + FAC
    shares = lax.all_to_all(shares, ("xh", "y", "xl"), 0, 0, axis_index_groups=[list(PLANE)])
    strip = call(
        sum_kernel,
        [VMEM],
        (4, 2 * STRIP, STRIP),
        BF16,
        [pltpu.VMEM((2 * STRIP, STRIP), BF16), pltpu.SemaphoreType.DMA((4,))],
        out=HBM,
    )(shares)
    strip, pack = lax.optimization_barrier((strip, pack))
    tables = (2 * STRIP, 4 * HALF)
    decode, spot = call(
        decode_kernel,
        [SMEM, VMEM],
        [(AHEAD, *tables), (8, STRIP)],
        [BF16, jnp.int32],
        turned_scratch,
        moved=3 << 20,
        out=[VMEM] * 2,
    )(column_place, pack)
    strips = lax.all_to_all(strip, line, 0, 0, axis_index_groups=gather)
    partial = call(
        subgrid_kernel,
        [VMEM] * 3,
        (8, STRIP, STRIP),
        BF16,
        [pltpu.VMEM((8 - AHEAD, *tables), BF16), *turned_scratch],
        flops=1 << 29,
    )(strips, decode, pack)
    received = lax.all_to_all(partial, line, 0, 0, axis_index_groups=reduce)
    subgrid = call(
        place_kernel,
        [VMEM, VMEM],
        (2, SUBGRID, STRIP),
        F32,
        [pltpu.VMEM((2, SUBGRID + STRIP, STRIP), F32), pltpu.SemaphoreType.DMA((2,))],
        out=HBM,
    )(spot, received)
    return subgrid.reshape(1, 1, 2, SUBGRID, STRIP)


def solution(mesh):
    split = Mesh(mesh.devices.reshape(SIZES), SPLIT)
    in_specs = (P(None, COL, FAC), P(COL), P(), P(), P(), P(), P())
    return jax.shard_map(
        on_device,
        mesh=split,
        in_specs=in_specs,
        out_specs=P(COL, FAC, None, None, None),
        check_vma=False,
    )
```

```python
import math

import jax
import jax.numpy as jnp
import numpy as np
from jax import lax
from jax.experimental import pallas as pl
from jax.experimental.pallas import tpu as pltpu
from jax.sharding import Mesh, PartitionSpec as P

FACET = 4096
STRIP = 128
SUBGRID = 512
HALF = 256
SPLIT = ("xh", "y", "core", "xl", "zh", "zl")
SIZES = (2, 4, 2, 2, 4, 4)
COL = SPLIT[:3]
FAC = SPLIT[3:]
PLANE = (13, 12, 15, 14, 9, 8, 11, 10, 5, 4, 7, 6, 1, 0, 3, 2)
RUN = (0, 1, 2, 3)
RUNS = ((2, 3, 1, 0), (2, 3, 1, 0))
TWIST = (0, 0, 2, 2)
MEMBERS = ((0, 0), (0, 1), (0, 2), (0, 3), (1, 0), (1, 1), (1, 2), (1, 3))
SHIFT = (2, 0)
F32 = jnp.float32
BF16 = jnp.bfloat16
VMEM = pl.BlockSpec(memory_space=pltpu.VMEM)
HBM = pl.BlockSpec(memory_space=pltpu.HBM)
SMEM = pl.BlockSpec(memory_space=pltpu.SMEM)
BASE = 48
ENCODE = slice(BASE, BASE + 8)
DECODE = slice(BASE + 8, BASE + 16)
OWN = slice(BASE + 16, BASE + 16 + HALF)
AHEAD = 6
NT = (((1,), (1,)), ((), ()))


def base_table():
    def rows(ks, scale):
        angle = (ks[:, None] * np.arange(HALF)[None, :] % FACET) * (2.0 * math.pi / FACET)
        return [np.cos(angle) * scale, -np.sin(angle) * scale]

    small, large = np.arange(16), 16 * np.arange(8)
    return np.concatenate(rows(small, 1.0) + rows(large, 1.0 / math.sqrt(FACET))).astype(np.float32)


def unit(phase):
    angle = phase.astype(F32) * (2.0 * math.pi / FACET)
    return jnp.cos(angle), -jnp.sin(angle)


def turned(pack_ref, turned_ref, block):
    k = lax.broadcasted_iota(jnp.int32, (16, HALF), 0)
    real, imag = unit((k * block & 15) * HALF)
    base_real, base_imag = pack_ref[0:16, :], pack_ref[16:32, :]
    real, imag = base_real * real - base_imag * imag, base_real * imag + base_imag * real
    for large in range(8):
        row_real = pack_ref[32 + large : 33 + large, :]
        row_imag = pack_ref[40 + large : 41 + large, :]
        rows = pl.ds(16 * large, 16)
        turned_ref[0, rows, :] = row_real * real - row_imag * imag
        turned_ref[1, rows, :] = row_real * imag + row_imag * real


def position():
    core, xl, zh, zl = (lax.axis_index(name) for name in ("core", "xl", "zh", "zl"))
    shift = jnp.where(core == 0, *SHIFT)
    place = (4 * zh + zl - shift) & 15
    return core, xl, place >> 2, place & 3, shift


def spread(starts):
    row = lax.broadcasted_iota(jnp.int32, (8, HALF), 0)
    first = jnp.zeros((8, HALF), jnp.int32)
    for n, start in enumerate(starts):
        first = jnp.where(row == n, start, first)
    return first.astype(F32)


def fill_tables(pack_ref, firsts, turn, blocks, outs, turned_ref):
    lane = lax.broadcasted_iota(jnp.int32, (8, HALF), 1)
    first = pack_ref[firsts].astype(jnp.int32)
    for c, block in enumerate(blocks):
        turned(pack_ref, turned_ref, block)
        real, imag = unit(first * (block * HALF + lane) & (FACET - 1))
        for k in range(0, STRIP, 16):
            rows = pl.ds(k, 16)
            base_real, base_imag = turned_ref[0, rows, :], turned_ref[1, rows, :]
            row = k // turn * 2 * turn + k % turn
            for n, out in outs.items():
                own_real, own_imag = real[n : n + 1], imag[n : n + 1]
                out[pl.ds(row, 16), HALF * c : HALF * (c + 1)] = (
                    own_real * base_real - own_imag * base_imag
                ).astype(BF16)
                out[pl.ds(row + turn, 16), HALF * c : HALF * (c + 1)] = (
                    own_real * base_imag + own_imag * base_real
                ).astype(BF16)


def prepare_kernel(
    facets_hbm,
    row_hbm,
    column_hbm,
    row_offset_hbm,
    offset_hbm,
    slot_hbm,
    base_hbm,
    out_hbm,
    first_hbm,
    pack_hbm,
    facets_ref,
    row_ref,
    column_ref,
    row_offset_ref,
    offset_ref,
    slot_ref,
    out_ref,
    pack_ref,
    sems,
    out_sems,
):
    core, xl, line, step, shift = position()
    pair = lax.axis_index("xh") * 4 + lax.axis_index("y")
    fac = (xl * 4 + lax.axis_index("zh")) * 4 + lax.axis_index("zl")
    copies = [
        pltpu.make_async_copy(source, target, sems.at[n])
        for n, (source, target) in enumerate(
            [
                (facets_hbm, facets_ref),
                (row_hbm, row_ref),
                (column_hbm, column_ref),
                (row_offset_hbm, row_offset_ref),
                (offset_hbm, offset_ref),
                (slot_hbm, slot_ref),
                (base_hbm, pack_ref.at[pl.ds(0, BASE)]),
            ]
        )
    ]
    for copy in copies:
        copy.start()
    for copy in copies[:3]:
        copy.wait()
    column = column_ref[pl.ds(fac, 1), :]
    for part in range(2):
        scaled = facets_ref[part].astype(F32) * column
        block = (scaled.T * row_ref[...]).astype(BF16)
        out_ref[STRIP * part : STRIP * (part + 1), :] = block
        pack_ref[BASE + 16 + STRIP * part : BASE + 16 + STRIP * (part + 1), :] = block.astype(F32)
    own_copy = pltpu.make_async_copy(out_ref, out_hbm, out_sems.at[0])
    own_copy.start()
    for copy in copies[3:6]:
        copy.wait()
    pack_ref[ENCODE] = spread([row_offset_ref[2 * n + core] for n in range(8)])
    slots = []
    twist = sum(jnp.where(line == n, TWIST[n], 0) for n in range(4))
    for first, second in zip(*RUNS):
        run = jnp.where(core == 0, first, second)
        away = jnp.where(core == 0, TWIST[first], TWIST[second])
        slots.append((4 * run + shift + ((step - twist + away) & 3)) & 15)
    slots = [slots[n] + 16 * side for side, n in MEMBERS]
    pack_ref[DECODE] = spread([offset_ref[slot_ref[2 * pair + core, slot] & 31] for slot in slots])
    copies[6].wait()
    first_copy = pltpu.make_async_copy(pack_ref, first_hbm, out_sems.at[1])
    first_copy.start()
    pack_copy = pltpu.make_async_copy(pack_ref.at[pl.ds(0, BASE + 16)], pack_hbm, out_sems.at[2])
    pack_copy.start()
    own_copy.wait()
    first_copy.wait()
    pack_copy.wait()


def encode_kernel(pack_ref, out_ref, turned_ref):
    core = lax.axis_index("core")
    pair = lax.axis_index("xh") * 4 + lax.axis_index("y")
    outs = {n: out_ref.at[n] for n in range(8)}
    blocks = [2 * pair + core, 2 * pair + 1 - core]
    fill_tables(pack_ref, ENCODE, STRIP // 2, blocks, outs, turned_ref)


def decode_tables(pack_ref, outs, turned_ref):
    _, _, line, _, shift = position()
    blocks = [8 * xl + ((2 * line + (shift >> 1) + half) & 7) for xl in range(2) for half in range(2)]
    fill_tables(pack_ref, DECODE, STRIP, blocks, outs, turned_ref)


def decode_kernel(place_ref, pack_ref, out_ref, spot_ref, turned_ref):
    spot_ref[...] = jnp.full((8, STRIP), place_ref[0], jnp.int32)
    decode_tables(pack_ref, {n: out_ref.at[n] for n in range(AHEAD)}, turned_ref)


def joined(real_rows, imag_rows):
    lane = lax.broadcasted_iota(jnp.int32, real_rows.shape, 1)
    turned = pltpu.roll(imag_rows, STRIP // 2, 1)
    return real_rows + jnp.where(lane < STRIP // 2, -turned, turned)


def strip_kernel(first_ref, other_ref, table_ref, out_ref):
    own = first_ref[OWN].astype(BF16)
    for n in range(8):
        product = lax.dot_general(
            own, table_ref[n, :, :HALF], NT, preferred_element_type=F32
        ) + lax.dot_general(
            other_ref[...], table_ref[n, :, HALF:], NT, preferred_element_type=F32
        )
        for half in range(2):
            part = product[:, STRIP * half : STRIP * (half + 1)]
            out_ref[PLANE.index(2 * n + half)] = joined(part[:STRIP], part[STRIP:]).astype(BF16)


def sum_kernel(parts_ref, out_hbm, total_ref, sems):
    for xl in range(2):
        first, *others = [PLANE.index(2 * n + xl) for n in range(8)]
        total = parts_ref[first].astype(F32)
        for n in others:
            total += parts_ref[n].astype(F32)
        total_ref[STRIP * xl : STRIP * (xl + 1), :] = total.astype(BF16)
    copies = [pltpu.make_async_copy(total_ref, out_hbm.at[n], sems.at[n]) for n in range(4)]
    for copy in copies:
        copy.start()
    for copy in copies:
        copy.wait()


def subgrid_kernel(strip_ref, ahead_ref, pack_ref, out_ref, late_ref, turned_ref):
    decode_tables(pack_ref, {n: late_ref.at[n - AHEAD] for n in range(AHEAD, 8)}, turned_ref)
    strip = jnp.concatenate(
        [
            strip_ref[RUN.index(n), STRIP * xl : STRIP * (xl + 1), :]
            for xl in range(2)
            for n in range(4)
        ]
    )
    for n in range(8):
        table = ahead_ref[n] if n < AHEAD else late_ref[n - AHEAD]
        product = jnp.dot(table, strip, preferred_element_type=F32)
        out_ref[n] = joined(product[:STRIP], product[STRIP:]).astype(BF16)


def place_kernel(place_ref, parts_ref, out_hbm, scratch_ref, sems):
    place = jnp.max(place_ref[...]) & (SUBGRID - 1)
    scratch_ref[...] = jnp.zeros_like(scratch_ref)
    halves = []
    for xl in range(2):
        first, *others = [n for n in range(8) if MEMBERS[n][0] == xl]
        total = parts_ref[first].astype(F32)
        for n in others:
            total += parts_ref[n].astype(F32)
        halves.append(total)
    low = lax.broadcasted_iota(jnp.int32, (STRIP, STRIP), 1) < STRIP // 2
    copies = []
    for part in range(2):
        turned = pltpu.roll(halves[1 - part], STRIP // 2, 1)
        whole = jnp.where(low, turned, halves[1]) if part else jnp.where(low, halves[0], turned)
        scratch_ref[part, pl.ds(place, STRIP), :] = whole
        scratch_ref[part, :STRIP, :] += scratch_ref[part, SUBGRID:, :]
        copy = pltpu.make_async_copy(
            scratch_ref.at[part, pl.ds(0, SUBGRID)], out_hbm.at[part], sems.at[part]
        )
        copy.start()
        copies.append(copy)
    for copy in copies:
        copy.wait()


def call(kernel, specs, shape, dtype, scratch=(), flops=0, moved=1 << 20, out=VMEM):
    if isinstance(shape, list):
        result = [jax.ShapeDtypeStruct(*pair) for pair in zip(shape, dtype)]
    else:
        result = jax.ShapeDtypeStruct(shape, dtype)
    return pl.pallas_call(
        kernel,
        out_shape=result,
        in_specs=specs,
        out_specs=out,
        scratch_shapes=list(scratch),
        compiler_params=pltpu.CompilerParams(vmem_limit_bytes=24 * 1024 * 1024),
        cost_estimate=pl.CostEstimate(flops=flops, bytes_accessed=moved, transcendentals=0),
    )


def prepare(*operands):
    return pl.pallas_call(
        prepare_kernel,
        out_shape=(
            jax.ShapeDtypeStruct((2 * STRIP, HALF), BF16),
            jax.ShapeDtypeStruct((BASE + 16 + HALF, HALF), F32),
            jax.ShapeDtypeStruct((BASE + 16, HALF), F32),
        ),
        in_specs=[HBM] * 7,
        out_specs=(HBM, HBM, HBM),
        scratch_shapes=[
            pltpu.VMEM((2, HALF, STRIP), BF16),
            pltpu.VMEM((1, HALF), F32),
            pltpu.VMEM((32, STRIP), F32),
            pltpu.SMEM((16,), jnp.int32),
            pltpu.SMEM((32,), jnp.int32),
            pltpu.SMEM((16, 32), jnp.int32),
            pltpu.VMEM((2 * STRIP, HALF), BF16),
            pltpu.VMEM((BASE + 16 + HALF, HALF), F32),
            pltpu.SemaphoreType.DMA((7,)),
            pltpu.SemaphoreType.DMA((3,)),
        ],
        compiler_params=pltpu.CompilerParams(vmem_limit_bytes=60 * 1024 * 1024),
        cost_estimate=pl.CostEstimate(flops=0, bytes_accessed=1 << 20, transcendentals=0),
    )(*operands)


def groups():
    gather = [
        [32 * core + 16 * xl + (4 * n + SHIFT[core] + j) % 16 for j in RUN]
        for core in range(2)
        for xl in range(2)
        for n in range(4)
    ]
    reduce = [
        [
            32 * core + 16 * xl + (4 * n + SHIFT[core] + (s + TWIST[n]) % 4) % 16
            for xl, n in ((xl, RUNS[core][n]) for xl, n in MEMBERS)
        ]
        for core in range(2)
        for s in range(4)
    ]
    return gather, reduce


def on_device(
    facets, row_taper, column_taper, column_place, row_offset, column_offset, slot_subgrid
):
    turned_scratch = [pltpu.VMEM((2, STRIP, HALF), F32)]
    own, first, pack = prepare(
        facets,
        row_taper.reshape(1, HALF),
        column_taper.reshape(32, STRIP),
        row_offset,
        column_offset,
        slot_subgrid,
        jnp.asarray(base_table()),
    )
    other = lax.ppermute(own, "core", [(0, 1), (1, 0)])
    encode = call(
        encode_kernel, [VMEM], (8, 2 * STRIP, 2 * HALF), BF16, turned_scratch, moved=3 << 20
    )(first)
    shares = call(strip_kernel, [VMEM] * 3, (16, STRIP, STRIP), BF16, flops=1 << 29)(
        first, other, encode
    )
    gather, reduce = groups()
    line = ("core",) + FAC
    shares = lax.all_to_all(shares, ("xh", "y", "xl"), 0, 0, axis_index_groups=[list(PLANE)])
    strip = call(
        sum_kernel,
        [VMEM],
        (4, 2 * STRIP, STRIP),
        BF16,
        [pltpu.VMEM((2 * STRIP, STRIP), BF16), pltpu.SemaphoreType.DMA((4,))],
        out=HBM,
    )(shares)
    strip, pack = lax.optimization_barrier((strip, pack))
    tables = (2 * STRIP, 4 * HALF)
    decode, spot = call(
        decode_kernel,
        [SMEM, VMEM],
        [(AHEAD, *tables), (8, STRIP)],
        [BF16, jnp.int32],
        turned_scratch,
        moved=3 << 20,
        out=[VMEM] * 2,
    )(column_place, pack)
    strips = lax.all_to_all(strip, line, 0, 0, axis_index_groups=gather)
    partial = call(
        subgrid_kernel,
        [VMEM] * 3,
        (8, STRIP, STRIP),
        BF16,
        [pltpu.VMEM((8 - AHEAD, *tables), BF16), *turned_scratch],
        flops=1 << 29,
    )(strips, decode, pack)
    received = lax.all_to_all(partial, line, 0, 0, axis_index_groups=reduce)
    subgrid = call(
        place_kernel,
        [VMEM, VMEM],
        (2, SUBGRID, STRIP),
        F32,
        [pltpu.VMEM((2, SUBGRID + STRIP, STRIP), F32), pltpu.SemaphoreType.DMA((2,))],
        out=HBM,
    )(spot, received)
    return subgrid.reshape(1, 1, 2, SUBGRID, STRIP)


def solution(mesh):
    split = Mesh(mesh.devices.reshape(SIZES), SPLIT)
    in_specs = (P(None, COL, FAC), P(COL), P(), P(), P(), P(), P())
    return jax.shard_map(
        on_device,
        mesh=split,
        in_specs=in_specs,
        out_specs=P(COL, FAC, None, None, None),
        check_vma=False,
    )
```
